32 devices in a mesh: pipe: 4 (over x, core), seq: 8 (over z, y).
Axes of the slice: x: 2, y: 2, z: 4, core: 2. Of those that a mesh axis runs over, the one named last changes fastest.
Arguments:
- layer_input: bfloat16 [4, 1024, 256], P('pipe', 'seq'), may hold values from -6 to 6
- filters: float32 [4, 1024, 256], P('pipe', 'seq'), may hold values from -1 to 1
- skip: float32 [4, 256], P('pipe'), may hold values from 0.5 to 1.5
- incoming: bfloat16 [4, 1024, 256], P('pipe', 'seq'), may hold values from -6 to 6
- loss_grad: bfloat16 [1024, 256], P('seq'), may hold values from -6 to 6
Outputs:
- input_grad: bfloat16 [4, 1024, 256], P('pipe', 'seq')
- filter_grad: float32 [4, 1024, 256], P('pipe', 'seq')
The draws below stay inside these ranges and needn't reach their ends.
All inputs are finite; a program needn't handle non-finite values.
Results may differ from the reference program's by a relative error of at most 0.001.
Values may be sent and summed in bfloat16 or wider, within the bound.
A program may use at most 64 MiB of HBM per device.

```python
import math
import jax
import jax.numpy as jnp
from jax import lax

CHAN = 256
SECTIONS = 4
SEQ = 1024


def draw_filters(key, part):
    key_rate = jax.random.fold_in(key, 11)
    key_noise = jax.random.fold_in(key, 12)
    log_rate = jax.random.uniform(key_rate, (SECTIONS, 1, CHAN), jnp.float32, math.log(0.5), math.log(SEQ / 40.0))
    rate = jnp.exp(log_rate)
    where_pos = lax.broadcasted_iota(jnp.int32, (1, SEQ, 1), 1).astype(jnp.float32) / SEQ
    window = jnp.exp(-rate * where_pos)
    energy = (1.0 - jnp.exp(-2.0 * rate)) / (1.0 - jnp.exp(-2.0 * rate / SEQ))
    noise = jax.random.truncated_normal(key_noise, -4.0, 4.0, (SECTIONS, SEQ, CHAN), jnp.float32)
    return noise * window / jnp.sqrt(energy)


def steps_of(stream_key, dims, pieces, low, top_value):
    level = 1.0
    for dim, parts in pieces:
        steps = jax.random.uniform(jax.random.fold_in(jax.random.fold_in(stream_key, 6), dim), (parts,), jnp.float32, low / len(pieces), top_value / len(pieces))
        level = level * jnp.repeat(jnp.exp(steps), dims[dim] // parts).reshape((-1,) + (1,) * (len(dims) - 1 - dim))
    return level


def scatter_about(own_key, shape, width, most, shards=(), kind=jnp.bfloat16):
    level = steps_of(own_key, shape, shards, -0.22, 0.18) if shards else 1.0
    result = jax.random.normal(own_key, shape, jnp.float32) * width * level
    return jnp.minimum(jnp.maximum(result, -most), most).astype(kind)


def setup_inputs(seed: int = 0) -> dict:
    key_of = jax.random.split(jax.random.key(seed), 6)
    return {
        "layer_input": scatter_about(key_of[0], (SECTIONS, SEQ, CHAN), 1.0, 6.0, ((0, 4), (1, 8))),
        "filters": draw_filters(jax.random.fold_in(key_of[5], 71), 0),
        "skip": jnp.clip(0.5 + 1.0 * jax.random.uniform(key_of[2], (SECTIONS, CHAN), jnp.float32) ** steps_of(key_of[2], (SECTIONS, CHAN), ((0, 4),), -0.2, 0.2), 0.5, 1.5),
        "incoming": scatter_about(key_of[3], (SECTIONS, SEQ, CHAN), 1.0, 6.0, ((0, 4), (1, 8))),
        "loss_grad": scatter_about(key_of[4], (SEQ, CHAN), 1.0, 6.0, ((0, 8),)),
    }


def section_grads(inputs, filt, grad_out, gain):
    size = 2 * SEQ
    u_spec = jnp.fft.rfft(inputs.astype(jnp.float32), n=size, axis=0)
    h_spec = jnp.fft.rfft(filt, n=size, axis=0)
    d_spec = jnp.fft.rfft(grad_out.astype(jnp.float32), n=size, axis=0)
    conv_grad = jnp.fft.irfft(jnp.conj(h_spec) * d_spec, n=size, axis=0)[:SEQ]
    filt_grad = jnp.fft.irfft(d_spec * jnp.conj(u_spec), n=size, axis=0)[:SEQ] * (1.0 / math.sqrt(SEQ))
    input_grad = (conv_grad + gain[None, :] * grad_out.astype(jnp.float32)).astype(jnp.bfloat16)
    return (input_grad, filt_grad.astype(jnp.float32))

def reference(layer_input, filters, skip, incoming, loss_grad):
    grads = []
    filt_grads = []
    for section in range(SECTIONS):
        if section + 1 < SECTIONS:
            grad_out = incoming[section + 1]
        else:
            grad_out = loss_grad
        one_grad, one_filt = section_grads(layer_input[section], filters[section], grad_out, skip[section])
        grads.append(one_grad)
        filt_grads.append(one_filt)
    return (jnp.stack(grads), jnp.stack(filt_grads))
```

```python
import functools
import math

import jax
import jax.numpy as jnp
from jax import lax
from jax.experimental import pallas as pl
from jax.experimental.pallas import tpu as pltpu
from jax.sharding import PartitionSpec as P

MESH = pl.DeviceIdType.MESH
HIGHEST = lax.Precision.HIGHEST


def passed_along(block, axis, distance):
    devices = range(lax.axis_size(axis))
    route = [(i - distance, i) for i in devices if i - distance in devices]
    return lax.ppermute(block, axis, route)


def angle_table(left, right, modulus):
    product = left * right % modulus
    angle = product.astype(jnp.float32) * (2.0 * math.pi / modulus)
    return (jnp.cos(angle), jnp.sin(angle))


def forward_spectrum(signals):
    parts = lax.axis_size("seq")
    rows = signals.shape[1]
    block = rows // parts
    total = 2 * parts * rows
    place = lax.axis_index("seq")
    gathered = lax.all_to_all(signals[:, None], "seq", split_axis=2, concat_axis=1, tiled=True)
    freq_ids = lax.broadcasted_iota(jnp.int32, (2 * parts, parts), 0)
    class_ids = lax.broadcasted_iota(jnp.int32, (2 * parts, parts), 1)
    cos_tab, sin_tab = angle_table(freq_ids, class_ids, 2 * parts)
    real = jnp.einsum("rq,kqjc->krjc", cos_tab, gathered, precision=HIGHEST)
    imag = -jnp.einsum("rq,kqjc->krjc", sin_tab, gathered, precision=HIGHEST)
    freq_grid = lax.broadcasted_iota(jnp.int32, (1, 2 * parts, block, 1), 1)
    row_grid = place * block + lax.broadcasted_iota(jnp.int32, (1, 2 * parts, block, 1), 2)
    tw_cos, tw_sin = angle_table(freq_grid, row_grid, total)
    segment_real = real * tw_cos + imag * tw_sin
    segment_imag = imag * tw_cos - real * tw_sin
    real = lax.all_to_all(segment_real, "seq", split_axis=1, concat_axis=2, tiled=True)
    imag = lax.all_to_all(segment_imag, "seq", split_axis=1, concat_axis=2, tiled=True)
    out_ids = lax.broadcasted_iota(jnp.int32, (rows, rows), 0)
    row_ids = lax.broadcasted_iota(jnp.int32, (rows, rows), 1)
    cos_tab, sin_tab = angle_table(out_ids, row_ids, rows)
    out_real = jnp.einsum("sj,kmjc->kmsc", cos_tab, real, precision=HIGHEST) + jnp.einsum(
        "sj,kmjc->kmsc", sin_tab, imag, precision=HIGHEST
    )
    out_imag = jnp.einsum("sj,kmjc->kmsc", cos_tab, imag, precision=HIGHEST) - jnp.einsum(
        "sj,kmjc->kmsc", sin_tab, real, precision=HIGHEST
    )
    return (out_real, out_imag)


def inverse_signal(real, imag):
    parts = lax.axis_size("seq")
    rows = real.shape[2]
    total = 2 * parts * rows
    place = lax.axis_index("seq")
    row_ids = lax.broadcasted_iota(jnp.int32, (rows, rows), 0)
    out_ids = lax.broadcasted_iota(jnp.int32, (rows, rows), 1)
    cos_tab, sin_tab = angle_table(row_ids, out_ids, rows)
    part_real = jnp.einsum("js,kmsc->kmjc", cos_tab, real, precision=HIGHEST) - jnp.einsum(
        "js,kmsc->kmjc", sin_tab, imag, precision=HIGHEST
    )
    part_imag = jnp.einsum("js,kmsc->kmjc", sin_tab, real, precision=HIGHEST) + jnp.einsum(
        "js,kmsc->kmjc", cos_tab, imag, precision=HIGHEST
    )
    freq_grid = 2 * place + lax.broadcasted_iota(jnp.int32, (1, 2, rows, 1), 1)
    row_grid = lax.broadcasted_iota(jnp.int32, (1, 2, rows, 1), 2)
    tw_cos, tw_sin = angle_table(freq_grid, row_grid, total)
    turned_real = part_real * tw_cos - part_imag * tw_sin
    turned_imag = part_real * tw_sin + part_imag * tw_cos
    gath_real = lax.all_to_all(turned_real, "seq", split_axis=2, concat_axis=1, tiled=True)
    gath_imag = lax.all_to_all(turned_imag, "seq", split_axis=2, concat_axis=1, tiled=True)
    class_ids = lax.broadcasted_iota(jnp.int32, (parts, 2 * parts), 0)
    freq_ids = lax.broadcasted_iota(jnp.int32, (parts, 2 * parts), 1)
    cos_q, sin_q = angle_table(class_ids, freq_ids, 2 * parts)
    factor = 1.0 / total
    value_real = (
        jnp.einsum("qr,krjc->kqjc", cos_q, gath_real, precision=HIGHEST)
        - jnp.einsum("qr,krjc->kqjc", sin_q, gath_imag, precision=HIGHEST)
    ) * factor
    return lax.all_to_all(value_real, "seq", split_axis=1, concat_axis=2, tiled=True)


def per_device(layer_input, filters, skip, incoming, loss_grad):
    received = passed_along(incoming, "pipe", -1)
    is_last = lax.axis_index("pipe") == lax.axis_size("pipe") - 1
    grad_out = jnp.where(is_last, loss_grad[None], received)
    rows = layer_input.shape[1]
    seq_total = rows * lax.axis_size("seq")
    inputs = layer_input[0].astype(jnp.float32)
    grad_vals = grad_out[0].astype(jnp.float32)
    spec_real, spec_imag = forward_spectrum(jnp.stack([inputs, filters[0], grad_vals]))
    in_real, filt_real, grad_real = (spec_real[0], spec_real[1], spec_real[2])
    in_imag, filt_imag, grad_imag = (spec_imag[0], spec_imag[1], spec_imag[2])
    scale = 1.0 / math.sqrt(seq_total)
    adj_real = filt_real * grad_real + filt_imag * grad_imag
    adj_imag = filt_real * grad_imag - filt_imag * grad_real
    corr_real = (grad_real * in_real + grad_imag * in_imag) * scale
    corr_imag = (grad_imag * in_real - grad_real * in_imag) * scale
    results = inverse_signal(jnp.stack([adj_real, corr_real]), jnp.stack([adj_imag, corr_imag]))
    conv_grad = results[0, 0]
    filt_grad = results[1, 0]
    input_grad = (conv_grad + skip[0][None, :] * grad_vals).astype(jnp.bfloat16)
    return (input_grad[None], filt_grad[None])


def remote(src, dst, send_sem, recv_sem, device):
    return pltpu.make_async_remote_copy(
        src_ref=src, dst_ref=dst, send_sem=send_sem, recv_sem=recv_sem, device_id=device, device_id_type=MESH
    )


def correlate_kernel(
    pipes, parts, x_ref, f_ref, skip_ref, inc_ref, loss_ref, ig_ref, fg_ref,
    x_out, f_out, g_out, x_in, g_in, f_pad, x_pad, g_val, conv, corr, conv_out, ig_in, fg_in,
    x_send, x_recv, f_send, f_recv, g_send, g_recv, ig_send, ig_recv, fg_send, fg_recv,
):
    section = lax.axis_index("pipe")
    me = lax.axis_index("seq")
    rows = x_ref.shape[0]
    chans = x_ref.shape[1] // parts
    before = lax.rem(section + pipes - 1, pipes)
    after = lax.rem(section + 1, pipes)
    others = [lax.rem(me + k, parts) for k in range(parts)]

    def part(ref, index, size=chans, start=0):
        return ref.at[pl.ds(pl.multiple_of(index * chans + start, 16), size)]

    barrier = pltpu.get_barrier_semaphore()
    for k in range(parts):
        if k:
            pl.semaphore_signal(barrier, inc=1, device_id=(section, others[k]), device_id_type=MESH)
        pl.semaphore_signal(barrier, inc=1, device_id=(after, others[k]), device_id_type=MESH)

    grad = jnp.where(section == 0, loss_ref[...].astype(jnp.float32), inc_ref[...].astype(jnp.float32))
    g_out[...] = grad.T.astype(jnp.bfloat16)
    row_ids = lax.broadcasted_iota(jnp.int32, (rows, rows), 0)
    col_ids = lax.broadcasted_iota(jnp.int32, (rows, rows), 1)
    flip = jnp.where(row_ids + col_ids == rows - 1, 1.0, 0.0).astype(jnp.bfloat16)
    x_out[...] = jnp.dot(flip, x_ref[...], preferred_element_type=jnp.float32).T.astype(jnp.bfloat16)
    filt = f_ref[...]
    filt_hi = filt.astype(jnp.bfloat16)
    filt_lo = (filt - filt_hi.astype(jnp.float32)).astype(jnp.bfloat16)
    f_out[...] = (
        jnp.dot(flip, filt_hi, preferred_element_type=jnp.float32)
        + jnp.dot(flip, filt_lo, preferred_element_type=jnp.float32)
    ).T
    half = parts * chans
    f_pad[half:, :] = jnp.zeros((half, rows), jnp.float32)
    x_pad[half:, :] = jnp.zeros((half, rows), jnp.float32)

    pl.semaphore_wait(barrier, 2 * parts - 1)

    sends = []
    for k in range(parts):
        to = others[k]
        sends.append(remote(part(g_out, to), part(g_in, me), g_send.at[k], g_recv.at[k], (before, to)))
        sends[-1].start()
    for k in range(1, parts):
        to = others[k]
        sends.append(remote(part(x_out, to), part(x_in, parts - 1 - me), x_send.at[k], x_recv.at[k], (section, to)))
        sends[-1].start()
        sends.append(remote(part(f_out, to), part(f_pad, parts - 1 - me), f_send.at[k], f_recv.at[k], (section, to)))
        sends[-1].start()
    part(f_pad, parts - 1 - me)[...] = part(f_out, me)[...]
    part(x_in, parts - 1 - me)[...] = part(x_out, me)[...]
    for copy in sends:
        copy.wait_recv()
    g_val[...] = g_in[...].astype(jnp.float32)
    x_pad[:half, :] = x_in[...].astype(jnp.float32)

    keep = col_ids <= row_ids

    def streams(ref, chan):
        pieces = [ref[pl.ds((parts - 1 - e) * chans + chan, parts, stride=chans), :] for e in range(parts)]
        return jnp.concatenate(pieces, axis=1)

    def hankel(chan):
        turned = []
        for e in range(parts):
            row = jnp.broadcast_to(g_val[pl.ds(e * chans + chan, 1), :], (rows, rows))
            turned.append(pltpu.roll(row, 1, 1, stride=1, stride_axis=0))
        turned.append(jnp.zeros((rows, rows), jnp.float32))
        return jnp.concatenate(
            [jnp.where(keep, turned[e], turned[e + 1]).astype(jnp.bfloat16) for e in range(parts)], axis=0
        )

    def pair(first):
        left, right = [], []
        for chan in (first, first + 1):
            filt = streams(f_pad, chan)
            hi = filt.astype(jnp.bfloat16).astype(jnp.float32)
            left += [hi, filt - hi, streams(x_pad, chan)]
            right.append(hankel(chan))
        result = jnp.dot(
            jnp.concatenate(left, axis=0).astype(jnp.bfloat16),
            jnp.concatenate(right, axis=1),
            preferred_element_type=jnp.float32,
        )
        for i in range(2):
            chan = first + i
            mine = result[3 * parts * i : 3 * parts * (i + 1), rows * i : rows * (i + 1)]
            where = pl.ds(chan, parts, stride=chans)
            gain = skip_ref[0, me * chans + chan]
            conv[where, :] = mine[:parts] + mine[parts : 2 * parts] + gain * g_val[where, :]
            corr[where, :] = mine[2 * parts :] * (1.0 / math.sqrt(rows * parts))

    returns = []
    size = chans // 2
    for h in range(2):
        def body(i, carry):
            pair(h * size + 2 * i)
            return carry

        lax.fori_loop(0, size // 2, body, 0)
        for a in range(parts):
            span = pl.ds(a * chans + h * size, size)
            conv_out[span, :] = conv[span, :].astype(jnp.bfloat16)
        for k in range(1, parts):
            to = others[k]
            sems = (ig_send.at[h, k], ig_recv.at[h, k])
            returns.append(
                remote(part(conv_out, to, size, h * size), part(ig_in, me, size, h * size), *sems, (section, to))
            )
            returns[-1].start()
            sems = (fg_send.at[h, k], fg_recv.at[h, k])
            returns.append(
                remote(part(corr, to, size, h * size), part(fg_in, me, size, h * size), *sems, (section, to))
            )
            returns[-1].start()
    part(ig_in, me)[...] = part(conv_out, me)[...]
    part(fg_in, me)[...] = part(corr, me)[...]
    for copy in returns:
        copy.wait_recv()
    ig_ref[...] = ig_in[...].astype(jnp.float32).T.astype(jnp.bfloat16)
    fg_ref[...] = fg_in[...].T
    for copy in sends + returns:
        copy.wait_send()


def kernel_per_device(pipes, parts, layer_input, filters, skip, incoming, loss_grad):
    rows, width = loss_grad.shape
    vmem = pl.BlockSpec(memory_space=pltpu.VMEM)
    narrow = pltpu.VMEM((width, rows), jnp.bfloat16)
    wide = pltpu.VMEM((width, rows), jnp.float32)
    padded = pltpu.VMEM((2 * width, rows), jnp.float32)
    sems = [pltpu.SemaphoreType.DMA((parts,))] * 6 + [pltpu.SemaphoreType.DMA((2, parts))] * 4
    input_grad, filter_grad = pl.pallas_call(
        functools.partial(correlate_kernel, pipes, parts),
        out_shape=(
            jax.ShapeDtypeStruct((rows, width), jnp.bfloat16),
            jax.ShapeDtypeStruct((rows, width), jnp.float32),
        ),
        in_specs=[vmem, vmem, pl.BlockSpec(memory_space=pltpu.SMEM), vmem, vmem],
        out_specs=(vmem, vmem),
        scratch_shapes=[narrow, wide, narrow, narrow, narrow, padded, padded, wide, wide, wide, narrow, narrow, wide]
        + sems,
        compiler_params=pltpu.CompilerParams(
            collective_id=0, has_side_effects=True, vmem_limit_bytes=32 * 1024 * 1024
        ),
    )(layer_input[0], filters[0], skip, incoming[0], loss_grad)
    return (input_grad[None], filter_grad[None])


def solution(mesh):
    pipes, parts = mesh.shape["pipe"], mesh.shape["seq"]

    def step(layer_input, filters, skip, incoming, loss_grad):
        rows, width = loss_grad.shape
        if pipes > 1 and parts == 8 and rows == 128 and width % (32 * parts) == 0:
            return kernel_per_device(pipes, parts, layer_input, filters, skip, incoming, loss_grad)
        return per_device(layer_input, filters, skip, incoming, loss_grad)

    return jax.shard_map(
        step,
        mesh=mesh,
        in_specs=(
            P("pipe", "seq", None),
            P("pipe", "seq", None),
            P("pipe", None),
            P("pipe", "seq", None),
            P("seq", None),
        ),
        out_specs=(P("pipe", "seq", None), P("pipe", "seq", None)),
        check_vma=False,
    )
```

```python
import functools
import math

import jax
import jax.numpy as jnp
from jax import lax
from jax.experimental import pallas as pl
from jax.experimental.pallas import tpu as pltpu
from jax.sharding import PartitionSpec as P

MESH = pl.DeviceIdType.MESH
HIGHEST = lax.Precision.HIGHEST


def passed_along(block, axis, distance):
    devices = range(lax.axis_size(axis))
    route = [(i - distance, i) for i in devices if i - distance in devices]
    return lax.ppermute(block, axis, route)


def angle_table(left, right, modulus):
    product = left * right % modulus
    angle = product.astype(jnp.float32) * (2.0 * math.pi / modulus)
    return (jnp.cos(angle), jnp.sin(angle))


def forward_spectrum(signals):
    parts = lax.axis_size("seq")
    rows = signals.shape[1]
    block = rows // parts
    total = 2 * parts * rows
    place = lax.axis_index("seq")
    gathered = lax.all_to_all(signals[:, None], "seq", split_axis=2, concat_axis=1, tiled=True)
    freq_ids = lax.broadcasted_iota(jnp.int32, (2 * parts, parts), 0)
    class_ids = lax.broadcasted_iota(jnp.int32, (2 * parts, parts), 1)
    cos_tab, sin_tab = angle_table(freq_ids, class_ids, 2 * parts)
    real = jnp.einsum("rq,kqjc->krjc", cos_tab, gathered, precision=HIGHEST)
    imag = -jnp.einsum("rq,kqjc->krjc", sin_tab, gathered, precision=HIGHEST)
    freq_grid = lax.broadcasted_iota(jnp.int32, (1, 2 * parts, block, 1), 1)
    row_grid = place * block + lax.broadcasted_iota(jnp.int32, (1, 2 * parts, block, 1), 2)
    tw_cos, tw_sin = angle_table(freq_grid, row_grid, total)
    segment_real = real * tw_cos + imag * tw_sin
    segment_imag = imag * tw_cos - real * tw_sin
    real = lax.all_to_all(segment_real, "seq", split_axis=1, concat_axis=2, tiled=True)
    imag = lax.all_to_all(segment_imag, "seq", split_axis=1, concat_axis=2, tiled=True)
    out_ids = lax.broadcasted_iota(jnp.int32, (rows, rows), 0)
    row_ids = lax.broadcasted_iota(jnp.int32, (rows, rows), 1)
    cos_tab, sin_tab = angle_table(out_ids, row_ids, rows)
    out_real = jnp.einsum("sj,kmjc->kmsc", cos_tab, real, precision=HIGHEST) + jnp.einsum(
        "sj,kmjc->kmsc", sin_tab, imag, precision=HIGHEST
    )
    out_imag = jnp.einsum("sj,kmjc->kmsc", cos_tab, imag, precision=HIGHEST) - jnp.einsum(
        "sj,kmjc->kmsc", sin_tab, real, precision=HIGHEST
    )
    return (out_real, out_imag)


def inverse_signal(real, imag):
    parts = lax.axis_size("seq")
    rows = real.shape[2]
    total = 2 * parts * rows
    place = lax.axis_index("seq")
    row_ids = lax.broadcasted_iota(jnp.int32, (rows, rows), 0)
    out_ids = lax.broadcasted_iota(jnp.int32, (rows, rows), 1)
    cos_tab, sin_tab = angle_table(row_ids, out_ids, rows)
    part_real = jnp.einsum("js,kmsc->kmjc", cos_tab, real, precision=HIGHEST) - jnp.einsum(
        "js,kmsc->kmjc", sin_tab, imag, precision=HIGHEST
    )
    part_imag = jnp.einsum("js,kmsc->kmjc", sin_tab, real, precision=HIGHEST) + jnp.einsum(
        "js,kmsc->kmjc", cos_tab, imag, precision=HIGHEST
    )
    freq_grid = 2 * place + lax.broadcasted_iota(jnp.int32, (1, 2, rows, 1), 1)
    row_grid = lax.broadcasted_iota(jnp.int32, (1, 2, rows, 1), 2)
    tw_cos, tw_sin = angle_table(freq_grid, row_grid, total)
    turned_real = part_real * tw_cos - part_imag * tw_sin
    turned_imag = part_real * tw_sin + part_imag * tw_cos
    gath_real = lax.all_to_all(turned_real, "seq", split_axis=2, concat_axis=1, tiled=True)
    gath_imag = lax.all_to_all(turned_imag, "seq", split_axis=2, concat_axis=1, tiled=True)
    class_ids = lax.broadcasted_iota(jnp.int32, (parts, 2 * parts), 0)
    freq_ids = lax.broadcasted_iota(jnp.int32, (parts, 2 * parts), 1)
    cos_q, sin_q = angle_table(class_ids, freq_ids, 2 * parts)
    factor = 1.0 / total
    value_real = (
        jnp.einsum("qr,krjc->kqjc", cos_q, gath_real, precision=HIGHEST)
        - jnp.einsum("qr,krjc->kqjc", sin_q, gath_imag, precision=HIGHEST)
    ) * factor
    return lax.all_to_all(value_real, "seq", split_axis=1, concat_axis=2, tiled=True)


def per_device(layer_input, filters, skip, incoming, loss_grad):
    received = passed_along(incoming, "pipe", -1)
    is_last = lax.axis_index("pipe") == lax.axis_size("pipe") - 1
    grad_out = jnp.where(is_last, loss_grad[None], received)
    rows = layer_input.shape[1]
    seq_total = rows * lax.axis_size("seq")
    inputs = layer_input[0].astype(jnp.float32)
    grad_vals = grad_out[0].astype(jnp.float32)
    spec_real, spec_imag = forward_spectrum(jnp.stack([inputs, filters[0], grad_vals]))
    in_real, filt_real, grad_real = (spec_real[0], spec_real[1], spec_real[2])
    in_imag, filt_imag, grad_imag = (spec_imag[0], spec_imag[1], spec_imag[2])
    scale = 1.0 / math.sqrt(seq_total)
    adj_real = filt_real * grad_real + filt_imag * grad_imag
    adj_imag = filt_real * grad_imag - filt_imag * grad_real
    corr_real = (grad_real * in_real + grad_imag * in_imag) * scale
    corr_imag = (grad_imag * in_real - grad_real * in_imag) * scale
    results = inverse_signal(jnp.stack([adj_real, corr_real]), jnp.stack([adj_imag, corr_imag]))
    conv_grad = results[0, 0]
    filt_grad = results[1, 0]
    input_grad = (conv_grad + skip[0][None, :] * grad_vals).astype(jnp.bfloat16)
    return (input_grad[None], filt_grad[None])


SIZE = 16


def remote(src, dst, send_sem, recv_sem, device):
    return pltpu.make_async_remote_copy(
        src_ref=src, dst_ref=dst, send_sem=send_sem, recv_sem=recv_sem, device_id=device, device_id_type=MESH
    )


def correlate_kernel(
    pipes, parts, x_hbm, f_hbm, skip_hbm, inc_hbm, loss_hbm, ig_ref, fg_ref,
    x_ref, f_ref, grad_ref, skip_ref, s_out, s_in, g_out, g_in, pads, g_val, conv, corr, r_out, r_in,
    load_sem, s_send, s_recv, g_send, g_recv, r_send, r_recv,
):
    section = lax.axis_index("pipe")
    me = lax.axis_index("seq")
    rows = x_ref.shape[0]
    chans = x_ref.shape[1] // parts
    chunks = chans // SIZE
    before = lax.rem(section + pipes - 1, pipes)
    after = lax.rem(section + 1, pipes)
    others = [lax.rem(me + k, parts) for k in range(parts)]

    @pl.when(section == 0)
    def _():
        pltpu.make_async_copy(loss_hbm, grad_ref, load_sem.at[0]).start()

    @pl.when(section != 0)
    def _():
        pltpu.make_async_copy(inc_hbm, grad_ref, load_sem.at[0]).start()

    load_f = pltpu.make_async_copy(f_hbm, f_ref, load_sem.at[1])
    load_x = pltpu.make_async_copy(x_hbm, x_ref, load_sem.at[2])
    load_skip = pltpu.make_async_copy(skip_hbm, skip_ref, load_sem.at[3])
    load_f.start()
    load_x.start()
    load_skip.start()

    barrier = pltpu.get_barrier_semaphore()
    for k in range(parts):
        if k:
            pl.semaphore_signal(barrier, inc=1, device_id=(section, others[k]), device_id_type=MESH)
        pl.semaphore_signal(barrier, inc=1, device_id=(after, others[k]), device_id_type=MESH)

    row_ids = lax.broadcasted_iota(jnp.int32, (rows, rows), 0)
    col_ids = lax.broadcasted_iota(jnp.int32, (rows, rows), 1)
    flip = jnp.where(row_ids + col_ids == rows - 1, 1.0, 0.0).astype(jnp.bfloat16)
    for kind in range(3):
        pads[kind, parts * chans :, :] = jnp.zeros((parts * chans, rows), jnp.float32)

    def turned_over(block):
        return jnp.dot(flip, block, preferred_element_type=jnp.float32).T.astype(jnp.bfloat16)

    def place(kind, block):
        for c in range(parts):
            for h in range(chunks):
                start = c * chans + h * SIZE
                s_out[c, h, kind * SIZE : (kind + 1) * SIZE, :] = block[start : start + SIZE]

    pltpu.make_async_copy(inc_hbm, grad_ref, load_sem.at[0]).wait()
    g_out[...] = grad_ref[...].astype(jnp.float32).T.astype(jnp.bfloat16)
    load_f.wait()
    filt = f_ref[...]
    filt_hi = filt.astype(jnp.bfloat16)
    place(0, turned_over(filt_hi))
    place(1, turned_over((filt - filt_hi.astype(jnp.float32)).astype(jnp.bfloat16)))
    load_x.wait()
    place(2, turned_over(x_ref[...]))

    pl.semaphore_wait(barrier, 2 * parts - 1)

    def span(index, h):
        return pl.ds(pl.multiple_of(index * chans + h * SIZE, SIZE), SIZE)

    slot = parts - 1 - me
    sends = []
    for h in range(chunks):
        group = []
        for k in range(parts):
            to = others[k]
            sems = (g_send.at[h, k], g_recv.at[h, k])
            group.append(remote(g_out.at[span(to, h)], g_in.at[span(me, h)], *sems, (before, to)))
            group[-1].start()
            if k:
                sems = (s_send.at[h, k], s_recv.at[h, k])
                group.append(remote(s_out.at[to, h], s_in.at[slot, h], *sems, (section, to)))
                group[-1].start()
        sends.append(group)
    s_in[slot] = s_out[me]
    load_skip.wait()

    keep = col_ids <= row_ids

    def streams(kind, chan):
        pieces = [
            pads[kind, pl.ds((parts - 1 - e) * chans + chan, parts, stride=chans), :] for e in range(parts)
        ]
        return jnp.concatenate(pieces, axis=1)

    def hankel(chan):
        turned = []
        for e in range(parts):
            row = jnp.broadcast_to(g_val[pl.ds(e * chans + chan, 1), :], (rows, rows))
            turned.append(pltpu.roll(row, 1, 1, stride=1, stride_axis=0))
        turned.append(jnp.zeros((rows, rows), jnp.float32))
        return jnp.concatenate(
            [jnp.where(keep, turned[e], turned[e + 1]).astype(jnp.bfloat16) for e in range(parts)], axis=0
        )

    def pair(first):
        left, right = [], []
        for chan in (first, first + 1):
            left += [streams(kind, chan) for kind in range(3)]
            right.append(hankel(chan))
        result = jnp.dot(
            jnp.concatenate(left, axis=0).astype(jnp.bfloat16),
            jnp.concatenate(right, axis=1),
            preferred_element_type=jnp.float32,
        )
        for i in range(2):
            chan = first + i
            mine = result[3 * parts * i : 3 * parts * (i + 1), rows * i : rows * (i + 1)]
            where = pl.ds(chan, parts, stride=chans)
            gain = skip_ref[0, me * chans + chan]
            conv[where, :] = mine[:parts] + mine[parts : 2 * parts] + gain * g_val[where, :]
            corr[where, :] = mine[2 * parts :] * (1.0 / math.sqrt(rows * parts))

    returns = []
    for h in range(chunks):
        for copy in sends[h]:
            copy.wait_recv()
        for e in range(parts):
            held = slice(e * chans + h * SIZE, e * chans + (h + 1) * SIZE)
            g_val[held, :] = g_in[held, :].astype(jnp.float32)
            for kind in range(3):
                pads[kind, held, :] = s_in[e, h, kind * SIZE : (kind + 1) * SIZE, :].astype(jnp.float32)

        def body(i, carry):
            pair(h * SIZE + 2 * i)
            return carry

        lax.fori_loop(0, SIZE // 2, body, 0, unroll=2)
        for a in range(parts):
            held = slice(a * chans + h * SIZE, a * chans + (h + 1) * SIZE)
            value = corr[held, :]
            value_hi = value.astype(jnp.bfloat16)
            r_out[a, h, :SIZE, :] = conv[held, :].astype(jnp.bfloat16)
            r_out[a, h, SIZE : 2 * SIZE, :] = value_hi
            r_out[a, h, 2 * SIZE :, :] = (value - value_hi.astype(jnp.float32)).astype(jnp.bfloat16)
        for k in range(1, parts):
            to = others[k]
            returns.append(remote(r_out.at[to, h], r_in.at[me, h], r_send.at[h, k], r_recv.at[h, k], (section, to)))
            returns[-1].start()
    r_in[me] = r_out[me]
    for copy in returns:
        copy.wait_recv()

    def gathered(kind):
        pieces = [
            r_in[c, h, kind * SIZE : (kind + 1) * SIZE, :].astype(jnp.float32)
            for c in range(parts)
            for h in range(chunks)
        ]
        return jnp.concatenate(pieces, axis=0)

    ig_ref[...] = gathered(0).T.astype(jnp.bfloat16)
    fg_ref[...] = (gathered(1) + gathered(2)).T
    for copy in sum(sends, returns):
        copy.wait_send()


def kernel_per_device(pipes, parts, layer_input, filters, skip, incoming, loss_grad):
    rows, width = loss_grad.shape
    chunks = width // parts // SIZE
    vmem = pl.BlockSpec(memory_space=pltpu.VMEM)
    hbm = pl.BlockSpec(memory_space=pltpu.HBM)
    narrow = pltpu.VMEM((width, rows), jnp.bfloat16)
    wide = pltpu.VMEM((width, rows), jnp.float32)
    triple = pltpu.VMEM((parts, chunks, 3 * SIZE, rows), jnp.bfloat16)
    sems = pltpu.SemaphoreType.DMA((chunks, parts))
    input_grad, filter_grad = pl.pallas_call(
        functools.partial(correlate_kernel, pipes, parts),
        out_shape=(
            jax.ShapeDtypeStruct((rows, width), jnp.bfloat16),
            jax.ShapeDtypeStruct((rows, width), jnp.float32),
        ),
        in_specs=[hbm] * 5,
        out_specs=(vmem, vmem),
        scratch_shapes=[
            pltpu.VMEM((rows, width), jnp.bfloat16),
            pltpu.VMEM((rows, width), jnp.float32),
            pltpu.VMEM((rows, width), jnp.bfloat16),
            pltpu.SMEM((1, width), jnp.float32),
            triple,
            triple,
            narrow,
            narrow,
            pltpu.VMEM((3, 2 * width, rows), jnp.float32),
            wide,
            wide,
            wide,
            triple,
            triple,
            pltpu.SemaphoreType.DMA((4,)),
        ]
        + [sems] * 6,
        compiler_params=pltpu.CompilerParams(
            collective_id=0, has_side_effects=True, vmem_limit_bytes=64 * 1024 * 1024 - 65536
        ),
    )(layer_input[0], filters[0], skip, incoming[0], loss_grad)
    return (input_grad[None], filter_grad[None])


def solution(mesh):
    pipes, parts = mesh.shape["pipe"], mesh.shape["seq"]

    def step(layer_input, filters, skip, incoming, loss_grad):
        rows, width = loss_grad.shape
        if pipes > 1 and parts == 8 and rows == 128 and width % (2 * SIZE * parts) == 0:
            return kernel_per_device(pipes, parts, layer_input, filters, skip, incoming, loss_grad)
        return per_device(layer_input, filters, skip, incoming, loss_grad)

    return jax.shard_map(
        step,
        mesh=mesh,
        in_specs=(
            P("pipe", "seq", None),
            P("pipe", "seq", None),
            P("pipe", None),
            P("pipe", "seq", None),
            P("seq", None),
        ),
        out_specs=(P("pipe", "seq", None), P("pipe", "seq", None)),
        check_vma=False,
    )
```

```python
import functools
import math

import jax
import jax.numpy as jnp
from jax import lax
from jax.experimental import pallas as pl
from jax.experimental.pallas import tpu as pltpu
from jax.sharding import PartitionSpec as P

MESH = pl.DeviceIdType.MESH
HIGHEST = lax.Precision.HIGHEST


def passed_along(block, axis, distance):
    devices = range(lax.axis_size(axis))
    route = [(i - distance, i) for i in devices if i - distance in devices]
    return lax.ppermute(block, axis, route)


def angle_table(left, right, modulus):
    product = left * right % modulus
    angle = product.astype(jnp.float32) * (2.0 * math.pi / modulus)
    return (jnp.cos(angle), jnp.sin(angle))


def forward_spectrum(signals):
    parts = lax.axis_size("seq")
    rows = signals.shape[1]
    block = rows // parts
    total = 2 * parts * rows
    place = lax.axis_index("seq")
    gathered = lax.all_to_all(signals[:, None], "seq", split_axis=2, concat_axis=1, tiled=True)
    freq_ids = lax.broadcasted_iota(jnp.int32, (2 * parts, parts), 0)
    class_ids = lax.broadcasted_iota(jnp.int32, (2 * parts, parts), 1)
    cos_tab, sin_tab = angle_table(freq_ids, class_ids, 2 * parts)
    real = jnp.einsum("rq,kqjc->krjc", cos_tab, gathered, precision=HIGHEST)
    imag = -jnp.einsum("rq,kqjc->krjc", sin_tab, gathered, precision=HIGHEST)
    freq_grid = lax.broadcasted_iota(jnp.int32, (1, 2 * parts, block, 1), 1)
    row_grid = place * block + lax.broadcasted_iota(jnp.int32, (1, 2 * parts, block, 1), 2)
    tw_cos, tw_sin = angle_table(freq_grid, row_grid, total)
    segment_real = real * tw_cos + imag * tw_sin
    segment_imag = imag * tw_cos - real * tw_sin
    real = lax.all_to_all(segment_real, "seq", split_axis=1, concat_axis=2, tiled=True)
    imag = lax.all_to_all(segment_imag, "seq", split_axis=1, concat_axis=2, tiled=True)
    out_ids = lax.broadcasted_iota(jnp.int32, (rows, rows), 0)
    row_ids = lax.broadcasted_iota(jnp.int32, (rows, rows), 1)
    cos_tab, sin_tab = angle_table(out_ids, row_ids, rows)
    out_real = jnp.einsum("sj,kmjc->kmsc", cos_tab, real, precision=HIGHEST) + jnp.einsum(
        "sj,kmjc->kmsc", sin_tab, imag, precision=HIGHEST
    )
    out_imag = jnp.einsum("sj,kmjc->kmsc", cos_tab, imag, precision=HIGHEST) - jnp.einsum(
        "sj,kmjc->kmsc", sin_tab, real, precision=HIGHEST
    )
    return (out_real, out_imag)


def inverse_signal(real, imag):
    parts = lax.axis_size("seq")
    rows = real.shape[2]
    total = 2 * parts * rows
    place = lax.axis_index("seq")
    row_ids = lax.broadcasted_iota(jnp.int32, (rows, rows), 0)
    out_ids = lax.broadcasted_iota(jnp.int32, (rows, rows), 1)
    cos_tab, sin_tab = angle_table(row_ids, out_ids, rows)
    part_real = jnp.einsum("js,kmsc->kmjc", cos_tab, real, precision=HIGHEST) - jnp.einsum(
        "js,kmsc->kmjc", sin_tab, imag, precision=HIGHEST
    )
    part_imag = jnp.einsum("js,kmsc->kmjc", sin_tab, real, precision=HIGHEST) + jnp.einsum(
        "js,kmsc->kmjc", cos_tab, imag, precision=HIGHEST
    )
    freq_grid = 2 * place + lax.broadcasted_iota(jnp.int32, (1, 2, rows, 1), 1)
    row_grid = lax.broadcasted_iota(jnp.int32, (1, 2, rows, 1), 2)
    tw_cos, tw_sin = angle_table(freq_grid, row_grid, total)
    turned_real = part_real * tw_cos - part_imag * tw_sin
    turned_imag = part_real * tw_sin + part_imag * tw_cos
    gath_real = lax.all_to_all(turned_real, "seq", split_axis=2, concat_axis=1, tiled=True)
    gath_imag = lax.all_to_all(turned_imag, "seq", split_axis=2, concat_axis=1, tiled=True)
    class_ids = lax.broadcasted_iota(jnp.int32, (parts, 2 * parts), 0)
    freq_ids = lax.broadcasted_iota(jnp.int32, (parts, 2 * parts), 1)
    cos_q, sin_q = angle_table(class_ids, freq_ids, 2 * parts)
    factor = 1.0 / total
    value_real = (
        jnp.einsum("qr,krjc->kqjc", cos_q, gath_real, precision=HIGHEST)
        - jnp.einsum("qr,krjc->kqjc", sin_q, gath_imag, precision=HIGHEST)
    ) * factor
    return lax.all_to_all(value_real, "seq", split_axis=1, concat_axis=2, tiled=True)


def per_device(layer_input, filters, skip, incoming, loss_grad):
    received = passed_along(incoming, "pipe", -1)
    is_last = lax.axis_index("pipe") == lax.axis_size("pipe") - 1
    grad_out = jnp.where(is_last, loss_grad[None], received)
    rows = layer_input.shape[1]
    seq_total = rows * lax.axis_size("seq")
    inputs = layer_input[0].astype(jnp.float32)
    grad_vals = grad_out[0].astype(jnp.float32)
    spec_real, spec_imag = forward_spectrum(jnp.stack([inputs, filters[0], grad_vals]))
    in_real, filt_real, grad_real = (spec_real[0], spec_real[1], spec_real[2])
    in_imag, filt_imag, grad_imag = (spec_imag[0], spec_imag[1], spec_imag[2])
    scale = 1.0 / math.sqrt(seq_total)
    adj_real = filt_real * grad_real + filt_imag * grad_imag
    adj_imag = filt_real * grad_imag - filt_imag * grad_real
    corr_real = (grad_real * in_real + grad_imag * in_imag) * scale
    corr_imag = (grad_imag * in_real - grad_real * in_imag) * scale
    results = inverse_signal(jnp.stack([adj_real, corr_real]), jnp.stack([adj_imag, corr_imag]))
    conv_grad = results[0, 0]
    filt_grad = results[1, 0]
    input_grad = (conv_grad + skip[0][None, :] * grad_vals).astype(jnp.bfloat16)
    return (input_grad[None], filt_grad[None])


SIZE = 16


def remote(src, dst, send_sem, recv_sem, device):
    return pltpu.make_async_remote_copy(
        src_ref=src, dst_ref=dst, send_sem=send_sem, recv_sem=recv_sem, device_id=device, device_id_type=MESH
    )


def correlate_kernel(
    pipes, parts, x_hbm, f_hbm, skip_hbm, inc_hbm, loss_hbm, r_in,
    x_ref, f_ref, grad_ref, skip_ref, s_out, s_in, g_out, g_in, pads, g_val, conv, corr, r_out,
    load_sem, s_send, s_recv, g_send, g_recv, r_send, r_recv,
):
    section = lax.axis_index("pipe")
    me = lax.axis_index("seq")
    rows = x_ref.shape[0]
    chans = x_ref.shape[1] // parts
    chunks = chans // SIZE
    before = lax.rem(section + pipes - 1, pipes)
    after = lax.rem(section + 1, pipes)
    others = [lax.rem(me + k, parts) for k in range(parts)]

    @pl.when(section == 0)
    def _():
        pltpu.make_async_copy(loss_hbm, grad_ref, load_sem.at[0]).start()

    @pl.when(section != 0)
    def _():
        pltpu.make_async_copy(inc_hbm, grad_ref, load_sem.at[0]).start()

    load_f = pltpu.make_async_copy(f_hbm, f_ref, load_sem.at[1])
    load_x = pltpu.make_async_copy(x_hbm, x_ref, load_sem.at[2])
    load_skip = pltpu.make_async_copy(skip_hbm, skip_ref, load_sem.at[3])
    load_f.start()
    load_x.start()
    load_skip.start()

    barrier = pltpu.get_barrier_semaphore()
    for k in range(parts):
        if k:
            pl.semaphore_signal(barrier, inc=1, device_id=(section, others[k]), device_id_type=MESH)
        pl.semaphore_signal(barrier, inc=1, device_id=(after, others[k]), device_id_type=MESH)

    row_ids = lax.broadcasted_iota(jnp.int32, (rows, rows), 0)
    col_ids = lax.broadcasted_iota(jnp.int32, (rows, rows), 1)
    flip = jnp.where(row_ids + col_ids == rows - 1, 1.0, 0.0).astype(jnp.bfloat16)
    for kind in range(3):
        pads[kind, parts * chans :, :] = jnp.zeros((parts * chans, rows), jnp.float32)

    def turned_over(block):
        return jnp.dot(flip, block, preferred_element_type=jnp.float32).T.astype(jnp.bfloat16)

    def place(kind, block):
        for c in range(parts):
            for h in range(chunks):
                start = c * chans + h * SIZE
                s_out[c, h, kind * SIZE : (kind + 1) * SIZE, :] = block[start : start + SIZE]

    pltpu.make_async_copy(inc_hbm, grad_ref, load_sem.at[0]).wait()
    g_out[...] = grad_ref[...].astype(jnp.float32).T.astype(jnp.bfloat16)
    load_f.wait()
    filt = f_ref[...]
    filt_hi = filt.astype(jnp.bfloat16)
    place(0, turned_over(filt_hi))
    place(1, turned_over((filt - filt_hi.astype(jnp.float32)).astype(jnp.bfloat16)))
    load_x.wait()
    place(2, turned_over(x_ref[...]))

    pl.semaphore_wait(barrier, 2 * parts - 1)

    def span(index, h):
        return pl.ds(pl.multiple_of(index * chans + h * SIZE, SIZE), SIZE)

    slot = parts - 1 - me
    sends = []
    for h in range(chunks):
        group = []
        for k in range(parts):
            to = others[k]
            sems = (g_send.at[h, k], g_recv.at[h, k])
            group.append(remote(g_out.at[span(to, h)], g_in.at[span(me, h)], *sems, (before, to)))
            group[-1].start()
            if k:
                sems = (s_send.at[h, k], s_recv.at[h, k])
                group.append(remote(s_out.at[to, h], s_in.at[slot, h], *sems, (section, to)))
                group[-1].start()
        sends.append(group)
    s_in[slot] = s_out[me]
    load_skip.wait()

    keep = col_ids <= row_ids

    def streams(kind, chan):
        pieces = [
            pads[kind, pl.ds((parts - 1 - e) * chans + chan, parts, stride=chans), :] for e in range(parts)
        ]
        return jnp.concatenate(pieces, axis=1)

    def hankel(chan):
        turned = []
        for e in range(parts):
            row = jnp.broadcast_to(g_val[pl.ds(e * chans + chan, 1), :], (rows, rows))
            turned.append(pltpu.roll(row, 1, 1, stride=1, stride_axis=0))
        turned.append(jnp.zeros((rows, rows), jnp.float32))
        return jnp.concatenate(
            [jnp.where(keep, turned[e], turned[e + 1]).astype(jnp.bfloat16) for e in range(parts)], axis=0
        )

    def pair(first):
        left, right = [], []
        for chan in (first, first + 1):
            left += [streams(kind, chan) for kind in range(3)]
            right.append(hankel(chan))
        result = jnp.dot(
            jnp.concatenate(left, axis=0).astype(jnp.bfloat16),
            jnp.concatenate(right, axis=1),
            preferred_element_type=jnp.float32,
        )
        for i in range(2):
            chan = first + i
            mine = result[3 * parts * i : 3 * parts * (i + 1), rows * i : rows * (i + 1)]
            where = pl.ds(chan, parts, stride=chans)
            gain = skip_ref[0, me * chans + chan]
            conv[where, :] = mine[:parts] + mine[parts : 2 * parts] + gain * g_val[where, :]
            corr[where, :] = mine[2 * parts :] * (1.0 / math.sqrt(rows * parts))

    returns = []
    for h in range(chunks):
        for copy in sends[h]:
            copy.wait_recv()
        for e in range(parts):
            held = slice(e * chans + h * SIZE, e * chans + (h + 1) * SIZE)
            g_val[held, :] = g_in[held, :].astype(jnp.float32)
            for kind in range(3):
                pads[kind, held, :] = s_in[e, h, kind * SIZE : (kind + 1) * SIZE, :].astype(jnp.float32)

        def body(i, carry):
            pair(h * SIZE + 2 * i)
            return carry

        lax.fori_loop(0, SIZE // 2, body, 0, unroll=2)
        for a in range(parts):
            held = slice(a * chans + h * SIZE, a * chans + (h + 1) * SIZE)
            value = corr[held, :]
            value_hi = value.astype(jnp.bfloat16)
            r_out[a, h, :SIZE, :] = conv[held, :].astype(jnp.bfloat16)
            r_out[a, h, SIZE : 2 * SIZE, :] = value_hi
            r_out[a, h, 2 * SIZE :, :] = (value - value_hi.astype(jnp.float32)).astype(jnp.bfloat16)
        for k in range(1, parts):
            to = others[k]
            returns.append(remote(r_out.at[to, h], r_in.at[me, h], r_send.at[h, k], r_recv.at[h, k], (section, to)))
            returns[-1].start()
    r_in[me] = r_out[me]
    for copy in returns:
        copy.wait_recv()

    for copy in sum(sends, returns):
        copy.wait_send()


def finish_kernel(r_ref, ig_ref, fg_ref):
    parts, chunks = r_ref.shape[:2]

    def gathered(kind):
        pieces = [
            r_ref[c, h, kind * SIZE : (kind + 1) * SIZE, :].astype(jnp.float32)
            for c in range(parts)
            for h in range(chunks)
        ]
        return jnp.concatenate(pieces, axis=0)

    ig_ref[...] = gathered(0).T.astype(jnp.bfloat16)
    fg_ref[...] = (gathered(1) + gathered(2)).T


def kernel_per_device(pipes, parts, layer_input, filters, skip, incoming, loss_grad):
    rows, width = loss_grad.shape
    chunks = width // parts // SIZE
    vmem = pl.BlockSpec(memory_space=pltpu.VMEM)
    hbm = pl.BlockSpec(memory_space=pl.ANY)
    narrow = pltpu.VMEM((width, rows), jnp.bfloat16)
    wide = pltpu.VMEM((width, rows), jnp.float32)
    triple = pltpu.VMEM((parts, chunks, 3 * SIZE, rows), jnp.bfloat16)
    sems = pltpu.SemaphoreType.DMA((chunks, parts))
    operands = (layer_input[0], filters[0], skip, incoming[0], loss_grad)
    returned = pl.pallas_call(
        functools.partial(correlate_kernel, pipes, parts),
        out_shape=pltpu.VMEM((parts, chunks, 3 * SIZE, rows), jnp.bfloat16),
        in_specs=[hbm] * 5,
        out_specs=vmem,
        scratch_shapes=[
            pltpu.VMEM((rows, width), jnp.bfloat16),
            pltpu.VMEM((rows, width), jnp.float32),
            pltpu.VMEM((rows, width), jnp.bfloat16),
            pltpu.SMEM((1, width), jnp.float32),
            triple,
            triple,
            narrow,
            narrow,
            pltpu.VMEM((3, 2 * width, rows), jnp.float32),
            wide,
            wide,
            wide,
            triple,
            pltpu.SemaphoreType.DMA((4,)),
        ]
        + [sems] * 6,
        compiler_params=pltpu.CompilerParams(
            collective_id=0, has_side_effects=True, vmem_limit_bytes=32 * 1024 * 1024
        ),
    )(*[pltpu.with_memory_space_constraint(operand, pltpu.HBM) for operand in operands])
    input_grad, filter_grad = pl.pallas_call(
        finish_kernel,
        out_shape=(
            jax.ShapeDtypeStruct((rows, width), jnp.bfloat16),
            jax.ShapeDtypeStruct((rows, width), jnp.float32),
        ),
        in_specs=[vmem],
        out_specs=(vmem, vmem),
    )(returned)
    return (input_grad[None], filter_grad[None])


def solution(mesh):
    pipes, parts = mesh.shape["pipe"], mesh.shape["seq"]

    def step(layer_input, filters, skip, incoming, loss_grad):
        rows, width = loss_grad.shape
        if pipes > 1 and parts == 8 and rows == 128 and width % (2 * SIZE * parts) == 0:
            return kernel_per_device(pipes, parts, layer_input, filters, skip, incoming, loss_grad)
        return per_device(layer_input, filters, skip, incoming, loss_grad)

    return jax.shard_map(
        step,
        mesh=mesh,
        in_specs=(
            P("pipe", "seq", None),
            P("pipe", "seq", None),
            P("pipe", None),
            P("pipe", "seq", None),
            P("seq", None),
        ),
        out_specs=(P("pipe", "seq", None), P("pipe", "seq", None)),
        check_vma=False,
    )
```

```python
import functools
import math

import jax
import jax.numpy as jnp
from jax import lax
from jax.experimental import pallas as pl
from jax.experimental.pallas import tpu as pltpu
from jax.sharding import PartitionSpec as P

MESH = pl.DeviceIdType.MESH
HIGHEST = lax.Precision.HIGHEST


def passed_along(block, axis, distance):
    devices = range(lax.axis_size(axis))
    route = [(i - distance, i) for i in devices if i - distance in devices]
    return lax.ppermute(block, axis, route)


def angle_table(left, right, modulus):
    product = left * right % modulus
    angle = product.astype(jnp.float32) * (2.0 * math.pi / modulus)
    return (jnp.cos(angle), jnp.sin(angle))


def forward_spectrum(signals):
    parts = lax.axis_size("seq")
    rows = signals.shape[1]
    block = rows // parts
    total = 2 * parts * rows
    place = lax.axis_index("seq")
    gathered = lax.all_to_all(signals[:, None], "seq", split_axis=2, concat_axis=1, tiled=True)
    freq_ids = lax.broadcasted_iota(jnp.int32, (2 * parts, parts), 0)
    class_ids = lax.broadcasted_iota(jnp.int32, (2 * parts, parts), 1)
    cos_tab, sin_tab = angle_table(freq_ids, class_ids, 2 * parts)
    real = jnp.einsum("rq,kqjc->krjc", cos_tab, gathered, precision=HIGHEST)
    imag = -jnp.einsum("rq,kqjc->krjc", sin_tab, gathered, precision=HIGHEST)
    freq_grid = lax.broadcasted_iota(jnp.int32, (1, 2 * parts, block, 1), 1)
    row_grid = place * block + lax.broadcasted_iota(jnp.int32, (1, 2 * parts, block, 1), 2)
    tw_cos, tw_sin = angle_table(freq_grid, row_grid, total)
    segment_real = real * tw_cos + imag * tw_sin
    segment_imag = imag * tw_cos - real * tw_sin
    real = lax.all_to_all(segment_real, "seq", split_axis=1, concat_axis=2, tiled=True)
    imag = lax.all_to_all(segment_imag, "seq", split_axis=1, concat_axis=2, tiled=True)
    out_ids = lax.broadcasted_iota(jnp.int32, (rows, rows), 0)
    row_ids = lax.broadcasted_iota(jnp.int32, (rows, rows), 1)
    cos_tab, sin_tab = angle_table(out_ids, row_ids, rows)
    out_real = jnp.einsum("sj,kmjc->kmsc", cos_tab, real, precision=HIGHEST) + jnp.einsum(
        "sj,kmjc->kmsc", sin_tab, imag, precision=HIGHEST
    )
    out_imag = jnp.einsum("sj,kmjc->kmsc", cos_tab, imag, precision=HIGHEST) - jnp.einsum(
        "sj,kmjc->kmsc", sin_tab, real, precision=HIGHEST
    )
    return (out_real, out_imag)


def inverse_signal(real, imag):
    parts = lax.axis_size("seq")
    rows = real.shape[2]
    total = 2 * parts * rows
    place = lax.axis_index("seq")
    row_ids = lax.broadcasted_iota(jnp.int32, (rows, rows), 0)
    out_ids = lax.broadcasted_iota(jnp.int32, (rows, rows), 1)
    cos_tab, sin_tab = angle_table(row_ids, out_ids, rows)
    part_real = jnp.einsum("js,kmsc->kmjc", cos_tab, real, precision=HIGHEST) - jnp.einsum(
        "js,kmsc->kmjc", sin_tab, imag, precision=HIGHEST
    )
    part_imag = jnp.einsum("js,kmsc->kmjc", sin_tab, real, precision=HIGHEST) + jnp.einsum(
        "js,kmsc->kmjc", cos_tab, imag, precision=HIGHEST
    )
    freq_grid = 2 * place + lax.broadcasted_iota(jnp.int32, (1, 2, rows, 1), 1)
    row_grid = lax.broadcasted_iota(jnp.int32, (1, 2, rows, 1), 2)
    tw_cos, tw_sin = angle_table(freq_grid, row_grid, total)
    turned_real = part_real * tw_cos - part_imag * tw_sin
    turned_imag = part_real * tw_sin + part_imag * tw_cos
    gath_real = lax.all_to_all(turned_real, "seq", split_axis=2, concat_axis=1, tiled=True)
    gath_imag = lax.all_to_all(turned_imag, "seq", split_axis=2, concat_axis=1, tiled=True)
    class_ids = lax.broadcasted_iota(jnp.int32, (parts, 2 * parts), 0)
    freq_ids = lax.broadcasted_iota(jnp.int32, (parts, 2 * parts), 1)
    cos_q, sin_q = angle_table(class_ids, freq_ids, 2 * parts)
    factor = 1.0 / total
    value_real = (
        jnp.einsum("qr,krjc->kqjc", cos_q, gath_real, precision=HIGHEST)
        - jnp.einsum("qr,krjc->kqjc", sin_q, gath_imag, precision=HIGHEST)
    ) * factor
    return lax.all_to_all(value_real, "seq", split_axis=1, concat_axis=2, tiled=True)


def per_device(layer_input, filters, skip, incoming, loss_grad):
    received = passed_along(incoming, "pipe", -1)
    is_last = lax.axis_index("pipe") == lax.axis_size("pipe") - 1
    grad_out = jnp.where(is_last, loss_grad[None], received)
    rows = layer_input.shape[1]
    seq_total = rows * lax.axis_size("seq")
    inputs = layer_input[0].astype(jnp.float32)
    grad_vals = grad_out[0].astype(jnp.float32)
    spec_real, spec_imag = forward_spectrum(jnp.stack([inputs, filters[0], grad_vals]))
    in_real, filt_real, grad_real = (spec_real[0], spec_real[1], spec_real[2])
    in_imag, filt_imag, grad_imag = (spec_imag[0], spec_imag[1], spec_imag[2])
    scale = 1.0 / math.sqrt(seq_total)
    adj_real = filt_real * grad_real + filt_imag * grad_imag
    adj_imag = filt_real * grad_imag - filt_imag * grad_real
    corr_real = (grad_real * in_real + grad_imag * in_imag) * scale
    corr_imag = (grad_imag * in_real - grad_real * in_imag) * scale
    results = inverse_signal(jnp.stack([adj_real, corr_real]), jnp.stack([adj_imag, corr_imag]))
    conv_grad = results[0, 0]
    filt_grad = results[1, 0]
    input_grad = (conv_grad + skip[0][None, :] * grad_vals).astype(jnp.bfloat16)
    return (input_grad[None], filt_grad[None])


SIZE = 16


def remote(src, dst, send_sem, recv_sem, device):
    return pltpu.make_async_remote_copy(
        src_ref=src, dst_ref=dst, send_sem=send_sem, recv_sem=recv_sem, device_id=device, device_id_type=MESH
    )


def correlate_kernel(
    pipes, parts, x_hbm, f_hbm, skip_hbm, inc_hbm, loss_hbm, r_in,
    x_ref, f_ref, grad_ref, skip_ref, s_out, s_in, g_out, g_in, pads, g_val, conv, corr, r_out,
    load_sem, s_send, s_recv, g_send, g_recv, r_send, r_recv,
):
    section = lax.axis_index("pipe")
    me = lax.axis_index("seq")
    rows = x_ref.shape[0]
    chans = x_ref.shape[1] // parts
    chunks = chans // SIZE
    before = lax.rem(section + pipes - 1, pipes)
    after = lax.rem(section + 1, pipes)
    others = [lax.rem(me + k, parts) for k in range(parts)]

    @pl.when(section == 0)
    def _():
        pltpu.make_async_copy(loss_hbm, grad_ref, load_sem.at[0]).start()

    @pl.when(section != 0)
    def _():
        pltpu.make_async_copy(inc_hbm, grad_ref, load_sem.at[0]).start()

    load_f = pltpu.make_async_copy(f_hbm, f_ref, load_sem.at[1])
    load_x = pltpu.make_async_copy(x_hbm, x_ref, load_sem.at[2])
    load_skip = pltpu.make_async_copy(skip_hbm, skip_ref, load_sem.at[3])
    load_f.start()
    load_x.start()
    load_skip.start()

    barrier = pltpu.get_barrier_semaphore()
    for k in range(parts):
        if k:
            pl.semaphore_signal(barrier, inc=1, device_id=(section, others[k]), device_id_type=MESH)
        pl.semaphore_signal(barrier, inc=1, device_id=(after, others[k]), device_id_type=MESH)

    row_ids = lax.broadcasted_iota(jnp.int32, (rows, rows), 0)
    col_ids = lax.broadcasted_iota(jnp.int32, (rows, rows), 1)
    flip = jnp.where(row_ids + col_ids == rows - 1, 1.0, 0.0).astype(jnp.bfloat16)
    for kind in range(3):
        pads[kind, parts * chans :, :] = jnp.zeros((parts * chans, rows), jnp.float32)

    def turned_over(block):
        return jnp.dot(flip, block, preferred_element_type=jnp.float32).T.astype(jnp.bfloat16)

    def place(kind, block):
        for c in range(parts):
            for h in range(chunks):
                start = c * chans + h * SIZE
                s_out[c, h, kind * SIZE : (kind + 1) * SIZE, :] = block[start : start + SIZE]

    pltpu.make_async_copy(inc_hbm, grad_ref, load_sem.at[0]).wait()
    g_out[...] = grad_ref[...].astype(jnp.float32).T.astype(jnp.bfloat16)
    load_f.wait()
    filt = f_ref[...]
    filt_hi = filt.astype(jnp.bfloat16)
    place(0, turned_over(filt_hi))
    place(1, turned_over((filt - filt_hi.astype(jnp.float32)).astype(jnp.bfloat16)))
    load_x.wait()
    place(2, turned_over(x_ref[...]))

    pl.semaphore_wait(barrier, 2 * parts - 1)

    def span(index, h):
        return pl.ds(pl.multiple_of(index * chans + h * SIZE, SIZE), SIZE)

    slot = parts - 1 - me
    sends = []
    for h in range(chunks):
        group = []
        for k in range(parts):
            to = others[k]
            sems = (g_send.at[h, k], g_recv.at[h, k])
            group.append(remote(g_out.at[span(to, h)], g_in.at[span(me, h)], *sems, (before, to)))
            group[-1].start()
            if k:
                sems = (s_send.at[h, k], s_recv.at[h, k])
                group.append(remote(s_out.at[to, h], s_in.at[slot, h], *sems, (section, to)))
                group[-1].start()
        sends.append(group)
    s_in[slot] = s_out[me]
    load_skip.wait()

    keep = col_ids <= row_ids

    def stream(kind, chan, e):
        return pads[kind, pl.ds((parts - 1 - e) * chans + chan, parts, stride=chans), :]

    def turned(chan, e):
        if e == parts:
            return jnp.zeros((rows, rows), jnp.float32)
        row = jnp.broadcast_to(g_val[pl.ds(e * chans + chan, 1), :], (rows, rows))
        return pltpu.roll(row, 1, 1, stride=1, stride_axis=0)

    def pair(first):
        both = (first, first + 1)
        later = [turned(chan, 0) for chan in both]
        result = jnp.zeros((6 * parts, 2 * rows), jnp.float32)
        for start in range(0, parts, 2):
            steps = (start, start + 1)
            left = [
                jnp.concatenate([stream(kind, chan, e) for e in steps], axis=1) for chan in both for kind in range(3)
            ]
            right = []
            for e in steps:
                blocks = []
                for i in range(2):
                    now, later[i] = later[i], turned(both[i], e + 1)
                    blocks.append(jnp.where(keep, now, later[i]).astype(jnp.bfloat16))
                right.append(jnp.concatenate(blocks, axis=1))
            result += jnp.dot(
                jnp.concatenate(left, axis=0).astype(jnp.bfloat16),
                jnp.concatenate(right, axis=0),
                preferred_element_type=jnp.float32,
            )
        for i in range(2):
            chan = first + i
            mine = result[3 * parts * i : 3 * parts * (i + 1), rows * i : rows * (i + 1)]
            where = pl.ds(chan, parts, stride=chans)
            gain = skip_ref[0, me * chans + chan]
            conv[where, :] = mine[:parts] + mine[parts : 2 * parts] + gain * g_val[where, :]
            corr[where, :] = mine[2 * parts :] * (1.0 / math.sqrt(rows * parts))

    returns = []
    for h in range(chunks):
        for copy in sends[h]:
            copy.wait_recv()
        for e in range(parts):
            held = slice(e * chans + h * SIZE, e * chans + (h + 1) * SIZE)
            g_val[held, :] = g_in[held, :].astype(jnp.float32)
            for kind in range(3):
                pads[kind, held, :] = s_in[e, h, kind * SIZE : (kind + 1) * SIZE, :].astype(jnp.float32)

        def body(i, carry):
            pair(h * SIZE + 2 * i)
            return carry

        lax.fori_loop(0, SIZE // 2, body, 0, unroll=4)
        for a in range(parts):
            held = slice(a * chans + h * SIZE, a * chans + (h + 1) * SIZE)
            value = corr[held, :]
            value_hi = value.astype(jnp.bfloat16)
            r_out[a, h, :SIZE, :] = conv[held, :].astype(jnp.bfloat16)
            r_out[a, h, SIZE : 2 * SIZE, :] = value_hi
            r_out[a, h, 2 * SIZE :, :] = (value - value_hi.astype(jnp.float32)).astype(jnp.bfloat16)
        for k in range(1, parts):
            to = others[k]
            returns.append(remote(r_out.at[to, h], r_in.at[me, h], r_send.at[h, k], r_recv.at[h, k], (section, to)))
            returns[-1].start()
    r_in[me] = r_out[me]
    for copy in returns:
        copy.wait_recv()

    for copy in sum(sends, returns):
        copy.wait_send()


def finish_kernel(r_ref, ig_hbm, fg_hbm, ig_ref, fg_ref, sems):
    parts, chunks = r_ref.shape[:2]

    def gathered(kind):
        pieces = [
            r_ref[c, h, kind * SIZE : (kind + 1) * SIZE, :].astype(jnp.float32)
            for c in range(parts)
            for h in range(chunks)
        ]
        return jnp.concatenate(pieces, axis=0)

    store_fg = pltpu.make_async_copy(fg_ref, fg_hbm, sems.at[0])
    store_ig = pltpu.make_async_copy(ig_ref, ig_hbm, sems.at[1])
    fg_ref[...] = (gathered(1) + gathered(2)).T
    store_fg.start()
    ig_ref[...] = gathered(0).T.astype(jnp.bfloat16)
    store_ig.start()
    store_fg.wait()
    store_ig.wait()


def kernel_per_device(pipes, parts, layer_input, filters, skip, incoming, loss_grad):
    rows, width = loss_grad.shape
    chunks = width // parts // SIZE
    vmem = pl.BlockSpec(memory_space=pltpu.VMEM)
    hbm = pl.BlockSpec(memory_space=pl.ANY)
    narrow = pltpu.VMEM((width, rows), jnp.bfloat16)
    wide = pltpu.VMEM((width, rows), jnp.float32)
    triple = pltpu.VMEM((parts, chunks, 3 * SIZE, rows), jnp.bfloat16)
    sems = pltpu.SemaphoreType.DMA((chunks, parts))
    operands = (layer_input[0], filters[0], skip, incoming[0], loss_grad)
    returned = pl.pallas_call(
        functools.partial(correlate_kernel, pipes, parts),
        out_shape=pltpu.VMEM((parts, chunks, 3 * SIZE, rows), jnp.bfloat16),
        in_specs=[hbm] * 5,
        out_specs=vmem,
        scratch_shapes=[
            pltpu.VMEM((rows, width), jnp.bfloat16),
            pltpu.VMEM((rows, width), jnp.float32),
            pltpu.VMEM((rows, width), jnp.bfloat16),
            pltpu.SMEM((1, width), jnp.float32),
            triple,
            triple,
            narrow,
            narrow,
            pltpu.VMEM((3, 2 * width, rows), jnp.float32),
            wide,
            wide,
            wide,
            triple,
            pltpu.SemaphoreType.DMA((4,)),
        ]
        + [sems] * 6,
        compiler_params=pltpu.CompilerParams(
            collective_id=0, has_side_effects=True, vmem_limit_bytes=32 * 1024 * 1024
        ),
    )(*[pltpu.with_memory_space_constraint(operand, pltpu.HBM) for operand in operands])
    input_grad, filter_grad = pl.pallas_call(
        finish_kernel,
        out_shape=(
            jax.ShapeDtypeStruct((rows, width), jnp.bfloat16),
            jax.ShapeDtypeStruct((rows, width), jnp.float32),
        ),
        in_specs=[vmem],
        out_specs=(hbm, hbm),
        scratch_shapes=[
            pltpu.VMEM((rows, width), jnp.bfloat16),
            pltpu.VMEM((rows, width), jnp.float32),
            pltpu.SemaphoreType.DMA((2,)),
        ],
        compiler_params=pltpu.CompilerParams(vmem_limit_bytes=8 * 1024 * 1024),
    )(returned)
    return (input_grad[None], filter_grad[None])


def solution(mesh):
    pipes, parts = mesh.shape["pipe"], mesh.shape["seq"]

    def step(layer_input, filters, skip, incoming, loss_grad):
        rows, width = loss_grad.shape
        if pipes > 1 and parts == 8 and rows == 128 and width % (2 * SIZE * parts) == 0:
            return kernel_per_device(pipes, parts, layer_input, filters, skip, incoming, loss_grad)
        return per_device(layer_input, filters, skip, incoming, loss_grad)

    return jax.shard_map(
        step,
        mesh=mesh,
        in_specs=(
            P("pipe", "seq", None),
            P("pipe", "seq", None),
            P("pipe", None),
            P("pipe", "seq", None),
            P("seq", None),
        ),
        out_specs=(P("pipe", "seq", None), P("pipe", "seq", None)),
        check_vma=False,
    )
```

```python
import functools
import math

import jax
import jax.numpy as jnp
from jax import lax
from jax.experimental import pallas as pl
from jax.experimental.pallas import tpu as pltpu
from jax.sharding import PartitionSpec as P

MESH = pl.DeviceIdType.MESH
HIGHEST = lax.Precision.HIGHEST


def passed_along(block, axis, distance):
    devices = range(lax.axis_size(axis))
    route = [(i - distance, i) for i in devices if i - distance in devices]
    return lax.ppermute(block, axis, route)


def angle_table(left, right, modulus):
    product = left * right % modulus
    angle = product.astype(jnp.float32) * (2.0 * math.pi / modulus)
    return (jnp.cos(angle), jnp.sin(angle))


def forward_spectrum(signals):
    parts = lax.axis_size("seq")
    rows = signals.shape[1]
    block = rows // parts
    total = 2 * parts * rows
    place = lax.axis_index("seq")
    gathered = lax.all_to_all(signals[:, None], "seq", split_axis=2, concat_axis=1, tiled=True)
    freq_ids = lax.broadcasted_iota(jnp.int32, (2 * parts, parts), 0)
    class_ids = lax.broadcasted_iota(jnp.int32, (2 * parts, parts), 1)
    cos_tab, sin_tab = angle_table(freq_ids, class_ids, 2 * parts)
    real = jnp.einsum("rq,kqjc->krjc", cos_tab, gathered, precision=HIGHEST)
    imag = -jnp.einsum("rq,kqjc->krjc", sin_tab, gathered, precision=HIGHEST)
    freq_grid = lax.broadcasted_iota(jnp.int32, (1, 2 * parts, block, 1), 1)
    row_grid = place * block + lax.broadcasted_iota(jnp.int32, (1, 2 * parts, block, 1), 2)
    tw_cos, tw_sin = angle_table(freq_grid, row_grid, total)
    segment_real = real * tw_cos + imag * tw_sin
    segment_imag = imag * tw_cos - real * tw_sin
    real = lax.all_to_all(segment_real, "seq", split_axis=1, concat_axis=2, tiled=True)
    imag = lax.all_to_all(segment_imag, "seq", split_axis=1, concat_axis=2, tiled=True)
    out_ids = lax.broadcasted_iota(jnp.int32, (rows, rows), 0)
    row_ids = lax.broadcasted_iota(jnp.int32, (rows, rows), 1)
    cos_tab, sin_tab = angle_table(out_ids, row_ids, rows)
    out_real = jnp.einsum("sj,kmjc->kmsc", cos_tab, real, precision=HIGHEST) + jnp.einsum(
        "sj,kmjc->kmsc", sin_tab, imag, precision=HIGHEST
    )
    out_imag = jnp.einsum("sj,kmjc->kmsc", cos_tab, imag, precision=HIGHEST) - jnp.einsum(
        "sj,kmjc->kmsc", sin_tab, real, precision=HIGHEST
    )
    return (out_real, out_imag)


def inverse_signal(real, imag):
    parts = lax.axis_size("seq")
    rows = real.shape[2]
    total = 2 * parts * rows
    place = lax.axis_index("seq")
    row_ids = lax.broadcasted_iota(jnp.int32, (rows, rows), 0)
    out_ids = lax.broadcasted_iota(jnp.int32, (rows, rows), 1)
    cos_tab, sin_tab = angle_table(row_ids, out_ids, rows)
    part_real = jnp.einsum("js,kmsc->kmjc", cos_tab, real, precision=HIGHEST) - jnp.einsum(
        "js,kmsc->kmjc", sin_tab, imag, precision=HIGHEST
    )
    part_imag = jnp.einsum("js,kmsc->kmjc", sin_tab, real, precision=HIGHEST) + jnp.einsum(
        "js,kmsc->kmjc", cos_tab, imag, precision=HIGHEST
    )
    freq_grid = 2 * place + lax.broadcasted_iota(jnp.int32, (1, 2, rows, 1), 1)
    row_grid = lax.broadcasted_iota(jnp.int32, (1, 2, rows, 1), 2)
    tw_cos, tw_sin = angle_table(freq_grid, row_grid, total)
    turned_real = part_real * tw_cos - part_imag * tw_sin
    turned_imag = part_real * tw_sin + part_imag * tw_cos
    gath_real = lax.all_to_all(turned_real, "seq", split_axis=2, concat_axis=1, tiled=True)
    gath_imag = lax.all_to_all(turned_imag, "seq", split_axis=2, concat_axis=1, tiled=True)
    class_ids = lax.broadcasted_iota(jnp.int32, (parts, 2 * parts), 0)
    freq_ids = lax.broadcasted_iota(jnp.int32, (parts, 2 * parts), 1)
    cos_q, sin_q = angle_table(class_ids, freq_ids, 2 * parts)
    factor = 1.0 / total
    value_real = (
        jnp.einsum("qr,krjc->kqjc", cos_q, gath_real, precision=HIGHEST)
        - jnp.einsum("qr,krjc->kqjc", sin_q, gath_imag, precision=HIGHEST)
    ) * factor
    return lax.all_to_all(value_real, "seq", split_axis=1, concat_axis=2, tiled=True)


def per_device(layer_input, filters, skip, incoming, loss_grad):
    received = passed_along(incoming, "pipe", -1)
    is_last = lax.axis_index("pipe") == lax.axis_size("pipe") - 1
    grad_out = jnp.where(is_last, loss_grad[None], received)
    rows = layer_input.shape[1]
    seq_total = rows * lax.axis_size("seq")
    inputs = layer_input[0].astype(jnp.float32)
    grad_vals = grad_out[0].astype(jnp.float32)
    spec_real, spec_imag = forward_spectrum(jnp.stack([inputs, filters[0], grad_vals]))
    in_real, filt_real, grad_real = (spec_real[0], spec_real[1], spec_real[2])
    in_imag, filt_imag, grad_imag = (spec_imag[0], spec_imag[1], spec_imag[2])
    scale = 1.0 / math.sqrt(seq_total)
    adj_real = filt_real * grad_real + filt_imag * grad_imag
    adj_imag = filt_real * grad_imag - filt_imag * grad_real
    corr_real = (grad_real * in_real + grad_imag * in_imag) * scale
    corr_imag = (grad_imag * in_real - grad_real * in_imag) * scale
    results = inverse_signal(jnp.stack([adj_real, corr_real]), jnp.stack([adj_imag, corr_imag]))
    conv_grad = results[0, 0]
    filt_grad = results[1, 0]
    input_grad = (conv_grad + skip[0][None, :] * grad_vals).astype(jnp.bfloat16)
    return (input_grad[None], filt_grad[None])


SIZE = 16


def remote(src, dst, send_sem, recv_sem, device):
    return pltpu.make_async_remote_copy(
        src_ref=src, dst_ref=dst, send_sem=send_sem, recv_sem=recv_sem, device_id=device, device_id_type=MESH
    )


def correlate_kernel(
    pipes, parts, x_hbm, f_hbm, skip_hbm, inc_hbm, loss_hbm, r_in,
    x_ref, f_ref, grad_ref, skip_ref, s_out, s_in, g_out, g_in, pads, g_val, conv, corr, r_out,
    load_sem, s_send, s_recv, g_send, g_recv, r_send, r_recv,
):
    section = lax.axis_index("pipe")
    me = lax.axis_index("seq")
    rows = x_ref.shape[0]
    chans = x_ref.shape[1] // parts
    chunks = chans // SIZE
    before = lax.rem(section + pipes - 1, pipes)
    after = lax.rem(section + 1, pipes)
    others = [lax.rem(me + k, parts) for k in range(parts)]

    @pl.when(section == 0)
    def _():
        pltpu.make_async_copy(loss_hbm, grad_ref, load_sem.at[0]).start()

    @pl.when(section != 0)
    def _():
        pltpu.make_async_copy(inc_hbm, grad_ref, load_sem.at[0]).start()

    load_f = pltpu.make_async_copy(f_hbm, f_ref, load_sem.at[1])
    load_x = pltpu.make_async_copy(x_hbm, x_ref, load_sem.at[2])
    load_skip = pltpu.make_async_copy(skip_hbm, skip_ref, load_sem.at[3])
    load_f.start()
    load_x.start()
    load_skip.start()

    barrier = pltpu.get_barrier_semaphore()
    for k in range(parts):
        if k:
            pl.semaphore_signal(barrier, inc=1, device_id=(section, others[k]), device_id_type=MESH)
        pl.semaphore_signal(barrier, inc=1, device_id=(after, others[k]), device_id_type=MESH)

    row_ids = lax.broadcasted_iota(jnp.int32, (rows, rows), 0)
    col_ids = lax.broadcasted_iota(jnp.int32, (rows, rows), 1)
    flip = jnp.where(row_ids + col_ids == rows - 1, 1.0, 0.0).astype(jnp.bfloat16)
    for kind in range(3):
        pads[kind, parts * chans :, :] = jnp.zeros((parts * chans, rows), jnp.float32)

    def turned_over(block):
        return jnp.dot(flip, block, preferred_element_type=jnp.float32).T.astype(jnp.bfloat16)

    def place(kind, block):
        for c in range(parts):
            for h in range(chunks):
                start = c * chans + h * SIZE
                s_out[c, h, kind * SIZE : (kind + 1) * SIZE, :] = block[start : start + SIZE]

    pltpu.make_async_copy(inc_hbm, grad_ref, load_sem.at[0]).wait()
    g_out[...] = grad_ref[...].astype(jnp.float32).T.astype(jnp.bfloat16)
    load_f.wait()
    filt = f_ref[...]
    filt_hi = filt.astype(jnp.bfloat16)
    place(0, turned_over(filt_hi))
    place(1, turned_over((filt - filt_hi.astype(jnp.float32)).astype(jnp.bfloat16)))
    load_x.wait()
    place(2, turned_over(x_ref[...]))

    pl.semaphore_wait(barrier, 2 * parts - 1)

    def span(index, h):
        return pl.ds(pl.multiple_of(index * chans + h * SIZE, SIZE), SIZE)

    slot = parts - 1 - me
    sends = []
    for h in range(chunks):
        group = []
        for k in range(parts):
            to = others[k]
            sems = (g_send.at[h, k], g_recv.at[h, k])
            group.append(remote(g_out.at[span(to, h)], g_in.at[span(me, h)], *sems, (before, to)))
            group[-1].start()
            if k:
                sems = (s_send.at[h, k], s_recv.at[h, k])
                group.append(remote(s_out.at[to, h], s_in.at[slot, h], *sems, (section, to)))
                group[-1].start()
        sends.append(group)
    s_in[slot] = s_out[me]
    load_skip.wait()

    keep = col_ids <= row_ids

    def stream(kind, chan, e):
        return pads[kind, pl.ds((parts - 1 - e) * chans + chan, parts, stride=chans), :]

    def turned(chan, e):
        if e == parts:
            return jnp.zeros((rows, rows), jnp.bfloat16)
        row = jnp.broadcast_to(g_val[pl.ds(e * chans + chan, 1), :].astype(jnp.bfloat16), (rows, rows))
        return pltpu.roll(row, 1, 1, stride=1, stride_axis=0)

    def pair(first):
        both = (first, first + 1)
        later = [turned(chan, 0) for chan in both]
        result = jnp.zeros((6 * parts, 2 * rows), jnp.float32)
        for start in range(0, parts, 2):
            steps = (start, start + 1)
            left = [
                jnp.concatenate([stream(kind, chan, e) for e in steps], axis=1) for chan in both for kind in range(3)
            ]
            right = []
            for e in steps:
                blocks = []
                for i in range(2):
                    now, later[i] = later[i], turned(both[i], e + 1)
                    blocks.append(jnp.where(keep, now, later[i]))
                right.append(jnp.concatenate(blocks, axis=1))
            result += jnp.dot(
                jnp.concatenate(left, axis=0).astype(jnp.bfloat16),
                jnp.concatenate(right, axis=0),
                preferred_element_type=jnp.float32,
            )
        for i in range(2):
            chan = first + i
            mine = result[3 * parts * i : 3 * parts * (i + 1), rows * i : rows * (i + 1)]
            where = pl.ds(chan, parts, stride=chans)
            gain = skip_ref[0, me * chans + chan]
            conv[where, :] = mine[:parts] + mine[parts : 2 * parts] + gain * g_val[where, :]
            corr[where, :] = mine[2 * parts :] * (1.0 / math.sqrt(rows * parts))

    returns = []
    for h in range(chunks):
        for copy in sends[h]:
            copy.wait_recv()
        for e in range(parts):
            held = slice(e * chans + h * SIZE, e * chans + (h + 1) * SIZE)
            g_val[held, :] = g_in[held, :].astype(jnp.float32)
            for kind in range(3):
                pads[kind, held, :] = s_in[e, h, kind * SIZE : (kind + 1) * SIZE, :].astype(jnp.float32)

        def body(i, carry):
            pair(h * SIZE + 2 * i)
            return carry

        lax.fori_loop(0, SIZE // 2, body, 0, unroll=4)
        for a in range(parts):
            held = slice(a * chans + h * SIZE, a * chans + (h + 1) * SIZE)
            value = corr[held, :]
            value_hi = value.astype(jnp.bfloat16)
            r_out[a, h, :SIZE, :] = conv[held, :].astype(jnp.bfloat16)
            r_out[a, h, SIZE : 2 * SIZE, :] = value_hi
            r_out[a, h, 2 * SIZE :, :] = (value - value_hi.astype(jnp.float32)).astype(jnp.bfloat16)
        for k in range(1, parts):
            to = others[k]
            returns.append(remote(r_out.at[to, h], r_in.at[me, h], r_send.at[h, k], r_recv.at[h, k], (section, to)))
            returns[-1].start()
    r_in[me] = r_out[me]
    for copy in returns:
        copy.wait_recv()

    for copy in sum(sends, returns):
        copy.wait_send()


def finish_kernel(r_ref, ig_hbm, fg_hbm, ig_ref, fg_ref, sems):
    parts, chunks = r_ref.shape[:2]

    def gathered(kind):
        pieces = [
            r_ref[c, h, kind * SIZE : (kind + 1) * SIZE, :].astype(jnp.float32)
            for c in range(parts)
            for h in range(chunks)
        ]
        return jnp.concatenate(pieces, axis=0)

    store_fg = pltpu.make_async_copy(fg_ref, fg_hbm, sems.at[0])
    store_ig = pltpu.make_async_copy(ig_ref, ig_hbm, sems.at[1])
    fg_ref[...] = (gathered(1) + gathered(2)).T
    store_fg.start()
    ig_ref[...] = gathered(0).T.astype(jnp.bfloat16)
    store_ig.start()
    store_fg.wait()
    store_ig.wait()


def kernel_per_device(pipes, parts, layer_input, filters, skip, incoming, loss_grad):
    rows, width = loss_grad.shape
    chunks = width // parts // SIZE
    vmem = pl.BlockSpec(memory_space=pltpu.VMEM)
    hbm = pl.BlockSpec(memory_space=pl.ANY)
    narrow = pltpu.VMEM((width, rows), jnp.bfloat16)
    wide = pltpu.VMEM((width, rows), jnp.float32)
    triple = pltpu.VMEM((parts, chunks, 3 * SIZE, rows), jnp.bfloat16)
    sems = pltpu.SemaphoreType.DMA((chunks, parts))
    operands = (layer_input[0], filters[0], skip, incoming[0], loss_grad)
    returned = pl.pallas_call(
        functools.partial(correlate_kernel, pipes, parts),
        out_shape=pltpu.VMEM((parts, chunks, 3 * SIZE, rows), jnp.bfloat16),
        in_specs=[hbm] * 5,
        out_specs=vmem,
        scratch_shapes=[
            pltpu.VMEM((rows, width), jnp.bfloat16),
            pltpu.VMEM((rows, width), jnp.float32),
            pltpu.VMEM((rows, width), jnp.bfloat16),
            pltpu.SMEM((1, width), jnp.float32),
            triple,
            triple,
            narrow,
            narrow,
            pltpu.VMEM((3, 2 * width, rows), jnp.float32),
            wide,
            wide,
            wide,
            triple,
            pltpu.SemaphoreType.DMA((4,)),
        ]
        + [sems] * 6,
        compiler_params=pltpu.CompilerParams(
            collective_id=0, has_side_effects=True, vmem_limit_bytes=32 * 1024 * 1024
        ),
    )(*[pltpu.with_memory_space_constraint(operand, pltpu.HBM) for operand in operands])
    input_grad, filter_grad = pl.pallas_call(
        finish_kernel,
        out_shape=(
            jax.ShapeDtypeStruct((rows, width), jnp.bfloat16),
            jax.ShapeDtypeStruct((rows, width), jnp.float32),
        ),
        in_specs=[vmem],
        out_specs=(hbm, hbm),
        scratch_shapes=[
            pltpu.VMEM((rows, width), jnp.bfloat16),
            pltpu.VMEM((rows, width), jnp.float32),
            pltpu.SemaphoreType.DMA((2,)),
        ],
        compiler_params=pltpu.CompilerParams(vmem_limit_bytes=8 * 1024 * 1024),
    )(returned)
    return (input_grad[None], filter_grad[None])


def solution(mesh):
    pipes, parts = mesh.shape["pipe"], mesh.shape["seq"]

    def step(layer_input, filters, skip, incoming, loss_grad):
        rows, width = loss_grad.shape
        if pipes > 1 and parts == 8 and rows == 128 and width % (2 * SIZE * parts) == 0:
            return kernel_per_device(pipes, parts, layer_input, filters, skip, incoming, loss_grad)
        return per_device(layer_input, filters, skip, incoming, loss_grad)

    return jax.shard_map(
        step,
        mesh=mesh,
        in_specs=(
            P("pipe", "seq", None),
            P("pipe", "seq", None),
            P("pipe", None),
            P("pipe", "seq", None),
            P("seq", None),
        ),
        out_specs=(P("pipe", "seq", None), P("pipe", "seq", None)),
        check_vma=False,
    )
```

```python
import functools
import math

import jax
import jax.numpy as jnp
from jax import lax
from jax.experimental import pallas as pl
from jax.experimental.pallas import tpu as pltpu
from jax.sharding import PartitionSpec as P

MESH = pl.DeviceIdType.MESH
HIGHEST = lax.Precision.HIGHEST


def passed_along(block, axis, distance):
    devices = range(lax.axis_size(axis))
    route = [(i - distance, i) for i in devices if i - distance in devices]
    return lax.ppermute(block, axis, route)


def angle_table(left, right, modulus):
    product = left * right % modulus
    angle = product.astype(jnp.float32) * (2.0 * math.pi / modulus)
    return (jnp.cos(angle), jnp.sin(angle))


def forward_spectrum(signals):
    parts = lax.axis_size("seq")
    rows = signals.shape[1]
    block = rows // parts
    total = 2 * parts * rows
    place = lax.axis_index("seq")
    gathered = lax.all_to_all(signals[:, None], "seq", split_axis=2, concat_axis=1, tiled=True)
    freq_ids = lax.broadcasted_iota(jnp.int32, (2 * parts, parts), 0)
    class_ids = lax.broadcasted_iota(jnp.int32, (2 * parts, parts), 1)
    cos_tab, sin_tab = angle_table(freq_ids, class_ids, 2 * parts)
    real = jnp.einsum("rq,kqjc->krjc", cos_tab, gathered, precision=HIGHEST)
    imag = -jnp.einsum("rq,kqjc->krjc", sin_tab, gathered, precision=HIGHEST)
    freq_grid = lax.broadcasted_iota(jnp.int32, (1, 2 * parts, block, 1), 1)
    row_grid = place * block + lax.broadcasted_iota(jnp.int32, (1, 2 * parts, block, 1), 2)
    tw_cos, tw_sin = angle_table(freq_grid, row_grid, total)
    segment_real = real * tw_cos + imag * tw_sin
    segment_imag = imag * tw_cos - real * tw_sin
    real = lax.all_to_all(segment_real, "seq", split_axis=1, concat_axis=2, tiled=True)
    imag = lax.all_to_all(segment_imag, "seq", split_axis=1, concat_axis=2, tiled=True)
    out_ids = lax.broadcasted_iota(jnp.int32, (rows, rows), 0)
    row_ids = lax.broadcasted_iota(jnp.int32, (rows, rows), 1)
    cos_tab, sin_tab = angle_table(out_ids, row_ids, rows)
    out_real = jnp.einsum("sj,kmjc->kmsc", cos_tab, real, precision=HIGHEST) + jnp.einsum(
        "sj,kmjc->kmsc", sin_tab, imag, precision=HIGHEST
    )
    out_imag = jnp.einsum("sj,kmjc->kmsc", cos_tab, imag, precision=HIGHEST) - jnp.einsum(
        "sj,kmjc->kmsc", sin_tab, real, precision=HIGHEST
    )
    return (out_real, out_imag)


def inverse_signal(real, imag):
    parts = lax.axis_size("seq")
    rows = real.shape[2]
    total = 2 * parts * rows
    place = lax.axis_index("seq")
    row_ids = lax.broadcasted_iota(jnp.int32, (rows, rows), 0)
    out_ids = lax.broadcasted_iota(jnp.int32, (rows, rows), 1)
    cos_tab, sin_tab = angle_table(row_ids, out_ids, rows)
    part_real = jnp.einsum("js,kmsc->kmjc", cos_tab, real, precision=HIGHEST) - jnp.einsum(
        "js,kmsc->kmjc", sin_tab, imag, precision=HIGHEST
    )
    part_imag = jnp.einsum("js,kmsc->kmjc", sin_tab, real, precision=HIGHEST) + jnp.einsum(
        "js,kmsc->kmjc", cos_tab, imag, precision=HIGHEST
    )
    freq_grid = 2 * place + lax.broadcasted_iota(jnp.int32, (1, 2, rows, 1), 1)
    row_grid = lax.broadcasted_iota(jnp.int32, (1, 2, rows, 1), 2)
    tw_cos, tw_sin = angle_table(freq_grid, row_grid, total)
    turned_real = part_real * tw_cos - part_imag * tw_sin
    turned_imag = part_real * tw_sin + part_imag * tw_cos
    gath_real = lax.all_to_all(turned_real, "seq", split_axis=2, concat_axis=1, tiled=True)
    gath_imag = lax.all_to_all(turned_imag, "seq", split_axis=2, concat_axis=1, tiled=True)
    class_ids = lax.broadcasted_iota(jnp.int32, (parts, 2 * parts), 0)
    freq_ids = lax.broadcasted_iota(jnp.int32, (parts, 2 * parts), 1)
    cos_q, sin_q = angle_table(class_ids, freq_ids, 2 * parts)
    factor = 1.0 / total
    value_real = (
        jnp.einsum("qr,krjc->kqjc", cos_q, gath_real, precision=HIGHEST)
        - jnp.einsum("qr,krjc->kqjc", sin_q, gath_imag, precision=HIGHEST)
    ) * factor
    return lax.all_to_all(value_real, "seq", split_axis=1, concat_axis=2, tiled=True)


def per_device(layer_input, filters, skip, incoming, loss_grad):
    received = passed_along(incoming, "pipe", -1)
    is_last = lax.axis_index("pipe") == lax.axis_size("pipe") - 1
    grad_out = jnp.where(is_last, loss_grad[None], received)
    rows = layer_input.shape[1]
    seq_total = rows * lax.axis_size("seq")
    inputs = layer_input[0].astype(jnp.float32)
    grad_vals = grad_out[0].astype(jnp.float32)
    spec_real, spec_imag = forward_spectrum(jnp.stack([inputs, filters[0], grad_vals]))
    in_real, filt_real, grad_real = (spec_real[0], spec_real[1], spec_real[2])
    in_imag, filt_imag, grad_imag = (spec_imag[0], spec_imag[1], spec_imag[2])
    scale = 1.0 / math.sqrt(seq_total)
    adj_real = filt_real * grad_real + filt_imag * grad_imag
    adj_imag = filt_real * grad_imag - filt_imag * grad_real
    corr_real = (grad_real * in_real + grad_imag * in_imag) * scale
    corr_imag = (grad_imag * in_real - grad_real * in_imag) * scale
    results = inverse_signal(jnp.stack([adj_real, corr_real]), jnp.stack([adj_imag, corr_imag]))
    conv_grad = results[0, 0]
    filt_grad = results[1, 0]
    input_grad = (conv_grad + skip[0][None, :] * grad_vals).astype(jnp.bfloat16)
    return (input_grad[None], filt_grad[None])


SIZE = 16
FINE = 32


def remote(src, dst, send_sem, recv_sem, device):
    return pltpu.make_async_remote_copy(
        src_ref=src, dst_ref=dst, send_sem=send_sem, recv_sem=recv_sem, device_id=device, device_id_type=MESH
    )


def correlate_kernel(
    pipes, parts, x_hbm, f_hbm, skip_hbm, inc_hbm, loss_hbm, r_in,
    x_ref, f_ref, grad_ref, skip_ref, s_out, s_in, g_out, g_in, pads, g_val, conv, corr, r_out,
    load_sem, s_send, s_recv, g_send, g_recv, r_send, r_recv,
):
    section = lax.axis_index("pipe")
    me = lax.axis_index("seq")
    rows = x_ref.shape[0]
    chans = x_ref.shape[1] // parts
    chunks = chans // SIZE
    before = lax.rem(section + pipes - 1, pipes)
    after = lax.rem(section + 1, pipes)
    others = [lax.rem(me + k, parts) for k in range(parts)]

    @pl.when(section == 0)
    def _():
        pltpu.make_async_copy(loss_hbm, grad_ref, load_sem.at[0]).start()

    @pl.when(section != 0)
    def _():
        pltpu.make_async_copy(inc_hbm, grad_ref, load_sem.at[0]).start()

    load_f = pltpu.make_async_copy(f_hbm, f_ref, load_sem.at[1])
    load_x = pltpu.make_async_copy(x_hbm, x_ref, load_sem.at[2])
    load_skip = pltpu.make_async_copy(skip_hbm, skip_ref, load_sem.at[3])
    load_f.start()
    load_x.start()
    load_skip.start()

    barrier = pltpu.get_barrier_semaphore()
    for k in range(parts):
        if k:
            pl.semaphore_signal(barrier, inc=1, device_id=(section, others[k]), device_id_type=MESH)
        pl.semaphore_signal(barrier, inc=1, device_id=(after, others[k]), device_id_type=MESH)

    row_ids = lax.broadcasted_iota(jnp.int32, (rows, rows), 0)
    col_ids = lax.broadcasted_iota(jnp.int32, (rows, rows), 1)
    flip = jnp.where(row_ids + col_ids == rows - 1, 1.0, 0.0).astype(jnp.bfloat16)

    def turned_over(block):
        return jnp.dot(flip, block, preferred_element_type=jnp.float32).T.astype(jnp.bfloat16)

    def place(kind, block):
        for c in range(parts):
            for h in range(chunks):
                start = c * chans + h * SIZE
                s_out[c, h, kind * SIZE : (kind + 1) * SIZE, :] = block[start : start + SIZE]

    pltpu.make_async_copy(inc_hbm, grad_ref, load_sem.at[0]).wait()
    g_out[...] = grad_ref[...].astype(jnp.float32).T.astype(jnp.bfloat16)
    load_f.wait()
    filt = f_ref[...]
    filt_hi = filt.astype(jnp.bfloat16)
    place(0, turned_over(filt_hi))
    place(1, turned_over((filt - filt_hi.astype(jnp.float32)).astype(jnp.bfloat16)))
    load_x.wait()
    place(2, turned_over(x_ref[...]))

    pl.semaphore_wait(barrier, 2 * parts - 1)

    def span(index, h):
        return pl.ds(pl.multiple_of(index * chans + h * SIZE, SIZE), SIZE)

    slot = parts - 1 - me
    sends = []
    for h in range(chunks):
        group = []
        for k in range(parts):
            to = others[k]
            sems = (g_send.at[h, k], g_recv.at[h, k])
            group.append(remote(g_out.at[span(to, h)], g_in.at[span(me, h)], *sems, (before, to)))
            group[-1].start()
            if k:
                sems = (s_send.at[h, k], s_recv.at[h, k])
                group.append(remote(s_out.at[to, h], s_in.at[slot, h], *sems, (section, to)))
                group[-1].start()
        sends.append(group)
    s_in[slot] = s_out[me]
    load_skip.wait()

    groups = rows // FINE
    lane = lax.broadcasted_iota(jnp.int32, (3 * SIZE, rows), 1) // FINE
    fine_row = lax.broadcasted_iota(jnp.int32, (FINE, rows), 0)
    fine_col = lax.broadcasted_iota(jnp.int32, (FINE, rows), 1)
    keep = fine_col + FINE - 1 - fine_row < rows
    wide_lane = lax.broadcasted_iota(jnp.int32, (parts, rows), 1)
    tiles = parts // groups

    def spread(h):
        nothing = jnp.zeros((3 * SIZE, rows), jnp.bfloat16)
        turns = []
        for e in range(parts):
            block = s_in[e, h]
            turns.append([block] + [pltpu.roll(block, FINE * r, 1) for r in range(1, groups)])
        for j in range(groups):
            for a in range(parts):
                for v in range(tiles):
                    value = nothing
                    for q in range(groups):
                        e = groups * v + q + a
                        if e < parts:
                            value = jnp.where(lane == q, turns[e][(q - j) % groups], value)
                    value = value.astype(jnp.float32)
                    for kind in range(3):
                        start = ((kind * groups + j) * parts + a) * SIZE
                        pads[v, start : start + SIZE, :] = value[kind * SIZE : (kind + 1) * SIZE]

    def turned(chan, e):
        row = jnp.broadcast_to(g_val[pl.ds(e * chans + chan, 1), :].astype(jnp.bfloat16), (FINE, rows))
        return pltpu.roll(row, rows - FINE + 1, 1, stride=1, stride_axis=0)

    def one(h, i):
        chan = h * SIZE + i
        nothing = jnp.zeros((FINE, rows), jnp.bfloat16)
        turns = [turned(chan, e) for e in range(parts)] + [nothing]
        blocks = [jnp.where(keep, turns[e], turns[e + 1]) for e in range(parts)] + [nothing]
        right = jnp.concatenate(
            [jnp.concatenate([blocks[e], blocks[e + 1]], axis=1) for e in reversed(range(parts))], axis=0
        )
        left = jnp.concatenate(
            [
                jnp.concatenate(
                    [pads[v, pl.ds(m * parts * SIZE + i, parts, stride=SIZE), :] for v in range(tiles)], axis=1
                )
                for m in range(3 * groups)
            ],
            axis=0,
        )
        result = jnp.dot(left.astype(jnp.bfloat16), right, preferred_element_type=jnp.float32)

        def folded(kinds):
            total = None
            for j in range(groups):
                begin = FINE * (groups - 1 - j)
                part = sum(result[(kind * groups + j) * parts : (kind * groups + j + 1) * parts] for kind in kinds)
                piece = part[:, :rows]
                if begin:
                    piece = jnp.where(wide_lane >= begin, piece, part[:, rows:])
                    piece = pltpu.roll(piece, rows - begin, 1)
                total = piece if total is None else total + piece
            return total

        where = pl.ds(chan, parts, stride=chans)
        gain = skip_ref[0, me * chans + chan]
        conv[where, :] = folded((0, 1)) + gain * g_val[where, :]
        corr[where, :] = folded((2,)) * (1.0 / math.sqrt(rows * parts))

    returns = []
    for h in range(chunks):
        for copy in sends[h]:
            copy.wait_recv()
        for e in range(parts):
            held = slice(e * chans + h * SIZE, e * chans + (h + 1) * SIZE)
            g_val[held, :] = g_in[held, :].astype(jnp.float32)
        spread(h)

        def body(i, carry):
            one(h, i)
            return carry

        lax.fori_loop(0, SIZE, body, 0, unroll=8)
        for a in range(parts):
            held = slice(a * chans + h * SIZE, a * chans + (h + 1) * SIZE)
            value = corr[held, :]
            value_hi = value.astype(jnp.bfloat16)
            r_out[a, h, :SIZE, :] = conv[held, :].astype(jnp.bfloat16)
            r_out[a, h, SIZE : 2 * SIZE, :] = value_hi
            r_out[a, h, 2 * SIZE :, :] = (value - value_hi.astype(jnp.float32)).astype(jnp.bfloat16)
        for k in range(1, parts):
            to = others[k]
            returns.append(remote(r_out.at[to, h], r_in.at[me, h], r_send.at[h, k], r_recv.at[h, k], (section, to)))
            returns[-1].start()
    r_in[me] = r_out[me]
    for copy in returns:
        copy.wait_recv()

    for copy in sum(sends, returns):
        copy.wait_send()


def finish_kernel(r_ref, ig_hbm, fg_hbm, ig_ref, fg_ref, sems):
    parts, chunks = r_ref.shape[:2]

    def gathered(kind):
        pieces = [
            r_ref[c, h, kind * SIZE : (kind + 1) * SIZE, :].astype(jnp.float32)
            for c in range(parts)
            for h in range(chunks)
        ]
        return jnp.concatenate(pieces, axis=0)

    store_fg = pltpu.make_async_copy(fg_ref, fg_hbm, sems.at[0])
    store_ig = pltpu.make_async_copy(ig_ref, ig_hbm, sems.at[1])
    fg_ref[...] = (gathered(1) + gathered(2)).T
    store_fg.start()
    ig_ref[...] = gathered(0).T.astype(jnp.bfloat16)
    store_ig.start()
    store_fg.wait()
    store_ig.wait()


def kernel_per_device(pipes, parts, layer_input, filters, skip, incoming, loss_grad):
    rows, width = loss_grad.shape
    chunks = width // parts // SIZE
    vmem = pl.BlockSpec(memory_space=pltpu.VMEM)
    hbm = pl.BlockSpec(memory_space=pl.ANY)
    narrow = pltpu.VMEM((width, rows), jnp.bfloat16)
    wide = pltpu.VMEM((width, rows), jnp.float32)
    triple = pltpu.VMEM((parts, chunks, 3 * SIZE, rows), jnp.bfloat16)
    sems = pltpu.SemaphoreType.DMA((chunks, parts))
    operands = (layer_input[0], filters[0], skip, incoming[0], loss_grad)
    returned = pl.pallas_call(
        functools.partial(correlate_kernel, pipes, parts),
        out_shape=pltpu.VMEM((parts, chunks, 3 * SIZE, rows), jnp.bfloat16),
        in_specs=[hbm] * 5,
        out_specs=vmem,
        scratch_shapes=[
            pltpu.VMEM((rows, width), jnp.bfloat16),
            pltpu.VMEM((rows, width), jnp.float32),
            pltpu.VMEM((rows, width), jnp.bfloat16),
            pltpu.SMEM((1, width), jnp.float32),
            triple,
            triple,
            narrow,
            narrow,
            pltpu.VMEM((parts * FINE // rows, 3 * (rows // FINE) * parts * SIZE, rows), jnp.float32),
            wide,
            wide,
            wide,
            triple,
            pltpu.SemaphoreType.DMA((4,)),
        ]
        + [sems] * 6,
        compiler_params=pltpu.CompilerParams(
            collective_id=0, has_side_effects=True, vmem_limit_bytes=32 * 1024 * 1024
        ),
    )(*[pltpu.with_memory_space_constraint(operand, pltpu.HBM) for operand in operands])
    input_grad, filter_grad = pl.pallas_call(
        finish_kernel,
        out_shape=(
            jax.ShapeDtypeStruct((rows, width), jnp.bfloat16),
            jax.ShapeDtypeStruct((rows, width), jnp.float32),
        ),
        in_specs=[vmem],
        out_specs=(hbm, hbm),
        scratch_shapes=[
            pltpu.VMEM((rows, width), jnp.bfloat16),
            pltpu.VMEM((rows, width), jnp.float32),
            pltpu.SemaphoreType.DMA((2,)),
        ],
        compiler_params=pltpu.CompilerParams(vmem_limit_bytes=8 * 1024 * 1024),
    )(returned)
    return (input_grad[None], filter_grad[None])


def solution(mesh):
    pipes, parts = mesh.shape["pipe"], mesh.shape["seq"]

    def step(layer_input, filters, skip, incoming, loss_grad):
        rows, width = loss_grad.shape
        if pipes > 1 and parts == 8 and rows == 128 and width % (2 * SIZE * parts) == 0:
            return kernel_per_device(pipes, parts, layer_input, filters, skip, incoming, loss_grad)
        return per_device(layer_input, filters, skip, incoming, loss_grad)

    return jax.shard_map(
        step,
        mesh=mesh,
        in_specs=(
            P("pipe", "seq", None),
            P("pipe", "seq", None),
            P("pipe", None),
            P("pipe", "seq", None),
            P("seq", None),
        ),
        out_specs=(P("pipe", "seq", None), P("pipe", "seq", None)),
        check_vma=False,
    )
```

```python
import functools
import math

import jax
import jax.numpy as jnp
from jax import lax
from jax.experimental import pallas as pl
from jax.experimental.pallas import tpu as pltpu
from jax.sharding import PartitionSpec as P

MESH = pl.DeviceIdType.MESH
HIGHEST = lax.Precision.HIGHEST


def passed_along(block, axis, distance):
    devices = range(lax.axis_size(axis))
    route = [(i - distance, i) for i in devices if i - distance in devices]
    return lax.ppermute(block, axis, route)


def angle_table(left, right, modulus):
    product = left * right % modulus
    angle = product.astype(jnp.float32) * (2.0 * math.pi / modulus)
    return (jnp.cos(angle), jnp.sin(angle))


def forward_spectrum(signals):
    parts = lax.axis_size("seq")
    rows = signals.shape[1]
    block = rows // parts
    total = 2 * parts * rows
    place = lax.axis_index("seq")
    gathered = lax.all_to_all(signals[:, None], "seq", split_axis=2, concat_axis=1, tiled=True)
    freq_ids = lax.broadcasted_iota(jnp.int32, (2 * parts, parts), 0)
    class_ids = lax.broadcasted_iota(jnp.int32, (2 * parts, parts), 1)
    cos_tab, sin_tab = angle_table(freq_ids, class_ids, 2 * parts)
    real = jnp.einsum("rq,kqjc->krjc", cos_tab, gathered, precision=HIGHEST)
    imag = -jnp.einsum("rq,kqjc->krjc", sin_tab, gathered, precision=HIGHEST)
    freq_grid = lax.broadcasted_iota(jnp.int32, (1, 2 * parts, block, 1), 1)
    row_grid = place * block + lax.broadcasted_iota(jnp.int32, (1, 2 * parts, block, 1), 2)
    tw_cos, tw_sin = angle_table(freq_grid, row_grid, total)
    segment_real = real * tw_cos + imag * tw_sin
    segment_imag = imag * tw_cos - real * tw_sin
    real = lax.all_to_all(segment_real, "seq", split_axis=1, concat_axis=2, tiled=True)
    imag = lax.all_to_all(segment_imag, "seq", split_axis=1, concat_axis=2, tiled=True)
    out_ids = lax.broadcasted_iota(jnp.int32, (rows, rows), 0)
    row_ids = lax.broadcasted_iota(jnp.int32, (rows, rows), 1)
    cos_tab, sin_tab = angle_table(out_ids, row_ids, rows)
    out_real = jnp.einsum("sj,kmjc->kmsc", cos_tab, real, precision=HIGHEST) + jnp.einsum(
        "sj,kmjc->kmsc", sin_tab, imag, precision=HIGHEST
    )
    out_imag = jnp.einsum("sj,kmjc->kmsc", cos_tab, imag, precision=HIGHEST) - jnp.einsum(
        "sj,kmjc->kmsc", sin_tab, real, precision=HIGHEST
    )
    return (out_real, out_imag)


def inverse_signal(real, imag):
    parts = lax.axis_size("seq")
    rows = real.shape[2]
    total = 2 * parts * rows
    place = lax.axis_index("seq")
    row_ids = lax.broadcasted_iota(jnp.int32, (rows, rows), 0)
    out_ids = lax.broadcasted_iota(jnp.int32, (rows, rows), 1)
    cos_tab, sin_tab = angle_table(row_ids, out_ids, rows)
    part_real = jnp.einsum("js,kmsc->kmjc", cos_tab, real, precision=HIGHEST) - jnp.einsum(
        "js,kmsc->kmjc", sin_tab, imag, precision=HIGHEST
    )
    part_imag = jnp.einsum("js,kmsc->kmjc", sin_tab, real, precision=HIGHEST) + jnp.einsum(
        "js,kmsc->kmjc", cos_tab, imag, precision=HIGHEST
    )
    freq_grid = 2 * place + lax.broadcasted_iota(jnp.int32, (1, 2, rows, 1), 1)
    row_grid = lax.broadcasted_iota(jnp.int32, (1, 2, rows, 1), 2)
    tw_cos, tw_sin = angle_table(freq_grid, row_grid, total)
    turned_real = part_real * tw_cos - part_imag * tw_sin
    turned_imag = part_real * tw_sin + part_imag * tw_cos
    gath_real = lax.all_to_all(turned_real, "seq", split_axis=2, concat_axis=1, tiled=True)
    gath_imag = lax.all_to_all(turned_imag, "seq", split_axis=2, concat_axis=1, tiled=True)
    class_ids = lax.broadcasted_iota(jnp.int32, (parts, 2 * parts), 0)
    freq_ids = lax.broadcasted_iota(jnp.int32, (parts, 2 * parts), 1)
    cos_q, sin_q = angle_table(class_ids, freq_ids, 2 * parts)
    factor = 1.0 / total
    value_real = (
        jnp.einsum("qr,krjc->kqjc", cos_q, gath_real, precision=HIGHEST)
        - jnp.einsum("qr,krjc->kqjc", sin_q, gath_imag, precision=HIGHEST)
    ) * factor
    return lax.all_to_all(value_real, "seq", split_axis=1, concat_axis=2, tiled=True)


def per_device(layer_input, filters, skip, incoming, loss_grad):
    received = passed_along(incoming, "pipe", -1)
    is_last = lax.axis_index("pipe") == lax.axis_size("pipe") - 1
    grad_out = jnp.where(is_last, loss_grad[None], received)
    rows = layer_input.shape[1]
    seq_total = rows * lax.axis_size("seq")
    inputs = layer_input[0].astype(jnp.float32)
    grad_vals = grad_out[0].astype(jnp.float32)
    spec_real, spec_imag = forward_spectrum(jnp.stack([inputs, filters[0], grad_vals]))
    in_real, filt_real, grad_real = (spec_real[0], spec_real[1], spec_real[2])
    in_imag, filt_imag, grad_imag = (spec_imag[0], spec_imag[1], spec_imag[2])
    scale = 1.0 / math.sqrt(seq_total)
    adj_real = filt_real * grad_real + filt_imag * grad_imag
    adj_imag = filt_real * grad_imag - filt_imag * grad_real
    corr_real = (grad_real * in_real + grad_imag * in_imag) * scale
    corr_imag = (grad_imag * in_real - grad_real * in_imag) * scale
    results = inverse_signal(jnp.stack([adj_real, corr_real]), jnp.stack([adj_imag, corr_imag]))
    conv_grad = results[0, 0]
    filt_grad = results[1, 0]
    input_grad = (conv_grad + skip[0][None, :] * grad_vals).astype(jnp.bfloat16)
    return (input_grad[None], filt_grad[None])


SIZE = 16
FINE = 32


def remote(src, dst, send_sem, recv_sem, device):
    return pltpu.make_async_remote_copy(
        src_ref=src, dst_ref=dst, send_sem=send_sem, recv_sem=recv_sem, device_id=device, device_id_type=MESH
    )


def correlate_kernel(
    pipes, parts, x_hbm, f_hbm, skip_hbm, inc_hbm, loss_hbm, r_in,
    x_ref, f_ref, grad_ref, skip_ref, s_out, s_in, g_out, g_in, pads, g_val, conv, corr, r_out,
    load_sem, s_send, s_recv, g_send, g_recv, r_send, r_recv,
):
    section = lax.axis_index("pipe")
    me = lax.axis_index("seq")
    rows = x_ref.shape[0]
    chans = x_ref.shape[1] // parts
    chunks = chans // SIZE
    before = lax.rem(section + pipes - 1, pipes)
    after = lax.rem(section + 1, pipes)
    others = [lax.rem(me + k, parts) for k in range(parts)]

    @pl.when(section == 0)
    def _():
        pltpu.make_async_copy(loss_hbm, grad_ref, load_sem.at[0]).start()

    @pl.when(section != 0)
    def _():
        pltpu.make_async_copy(inc_hbm, grad_ref, load_sem.at[0]).start()

    load_f = pltpu.make_async_copy(f_hbm, f_ref, load_sem.at[1])
    load_x = pltpu.make_async_copy(x_hbm, x_ref, load_sem.at[2])
    load_skip = pltpu.make_async_copy(skip_hbm, skip_ref, load_sem.at[3])
    load_f.start()
    load_x.start()
    load_skip.start()

    barrier = pltpu.get_barrier_semaphore()
    for k in range(parts):
        if k:
            pl.semaphore_signal(barrier, inc=1, device_id=(section, others[k]), device_id_type=MESH)
        pl.semaphore_signal(barrier, inc=1, device_id=(after, others[k]), device_id_type=MESH)

    far_first = sorted(range(1, parts), key=lambda k: abs(k - parts // 2))
    slot = parts - 1 - me

    def block_of(index):
        return pl.ds(pl.multiple_of(index * chans, SIZE), chans)

    pltpu.make_async_copy(inc_hbm, grad_ref, load_sem.at[0]).wait()
    g_out[...] = grad_ref[...].astype(jnp.float32).T.astype(jnp.bfloat16)

    pl.semaphore_wait(barrier, 2 * parts - 1)

    g_sends = []
    for k in far_first + [0]:
        to = others[k]
        g_sends.append(
            remote(g_out.at[block_of(to)], g_in.at[block_of(me)], g_send.at[k], g_recv.at[k], (before, to))
        )
        g_sends[-1].start()

    row_ids = lax.broadcasted_iota(jnp.int32, (rows, rows), 0)
    col_ids = lax.broadcasted_iota(jnp.int32, (rows, rows), 1)
    flip = jnp.where(row_ids + col_ids == rows - 1, 1.0, 0.0).astype(jnp.bfloat16)

    def turned_over(block):
        return jnp.dot(flip, block, preferred_element_type=jnp.float32).T.astype(jnp.bfloat16)

    def place(kind, block):
        for c in range(parts):
            for h in range(chunks):
                start = c * chans + h * SIZE
                s_out[c, h, kind * SIZE : (kind + 1) * SIZE, :] = block[start : start + SIZE]

    load_f.wait()
    filt = f_ref[...]
    filt_hi = filt.astype(jnp.bfloat16)
    place(0, turned_over(filt_hi))
    place(1, turned_over((filt - filt_hi.astype(jnp.float32)).astype(jnp.bfloat16)))
    load_x.wait()
    place(2, turned_over(x_ref[...]))

    sends = []
    for h in range(chunks):
        group = []
        for k in far_first:
            to = others[k]
            sems = (s_send.at[h, k], s_recv.at[h, k])
            group.append(remote(s_out.at[to, h], s_in.at[slot, h], *sems, (section, to)))
            group[-1].start()
        sends.append(group)
    s_in[slot] = s_out[me]
    load_skip.wait()
    for copy in g_sends:
        copy.wait_recv()
    g_val[...] = g_in[...].astype(jnp.float32)

    groups = rows // FINE
    lane = lax.broadcasted_iota(jnp.int32, (3 * SIZE, rows), 1) // FINE
    fine_row = lax.broadcasted_iota(jnp.int32, (FINE, rows), 0)
    fine_col = lax.broadcasted_iota(jnp.int32, (FINE, rows), 1)
    keep = fine_col + FINE - 1 - fine_row < rows
    wide_lane = lax.broadcasted_iota(jnp.int32, (parts, rows), 1)
    tiles = parts // groups

    def spread(h):
        nothing = jnp.zeros((3 * SIZE, rows), jnp.bfloat16)
        turns = []
        for e in range(parts):
            block = s_in[e, h]
            turns.append([block] + [pltpu.roll(block, FINE * r, 1) for r in range(1, groups)])
        for j in range(groups):
            for a in range(parts):
                for v in range(tiles):
                    value = nothing
                    for q in range(groups):
                        e = groups * v + q + a
                        if e < parts:
                            value = jnp.where(lane == q, turns[e][(q - j) % groups], value)
                    value = value.astype(jnp.float32)
                    for kind in range(3):
                        start = ((kind * groups + j) * parts + a) * SIZE
                        pads[v, start : start + SIZE, :] = value[kind * SIZE : (kind + 1) * SIZE]

    def turned(chan, e):
        row = jnp.broadcast_to(g_val[pl.ds(e * chans + chan, 1), :].astype(jnp.bfloat16), (FINE, rows))
        return pltpu.roll(row, rows - FINE + 1, 1, stride=1, stride_axis=0)

    def one(h, i):
        chan = h * SIZE + i
        nothing = jnp.zeros((FINE, rows), jnp.bfloat16)
        turns = [turned(chan, e) for e in range(parts)] + [nothing]
        blocks = [jnp.where(keep, turns[e], turns[e + 1]) for e in range(parts)] + [nothing]
        right = jnp.concatenate(
            [jnp.concatenate([blocks[e], blocks[e + 1]], axis=1) for e in reversed(range(parts))], axis=0
        )
        left = jnp.concatenate(
            [
                jnp.concatenate(
                    [pads[v, pl.ds(m * parts * SIZE + i, parts, stride=SIZE), :] for v in range(tiles)], axis=1
                )
                for m in range(3 * groups)
            ],
            axis=0,
        )
        result = jnp.dot(left.astype(jnp.bfloat16), right, preferred_element_type=jnp.float32)

        def folded(kinds):
            total = None
            for j in range(groups):
                begin = FINE * (groups - 1 - j)
                part = sum(result[(kind * groups + j) * parts : (kind * groups + j + 1) * parts] for kind in kinds)
                piece = part[:, :rows]
                if begin:
                    piece = jnp.where(wide_lane >= begin, piece, part[:, rows:])
                    piece = pltpu.roll(piece, rows - begin, 1)
                total = piece if total is None else total + piece
            return total

        where = pl.ds(chan, parts, stride=chans)
        gain = skip_ref[0, me * chans + chan]
        conv[where, :] = folded((0, 1)) + gain * g_val[where, :]
        corr[where, :] = folded((2,)) * (1.0 / math.sqrt(rows * parts))

    returns = []
    for h in range(chunks):
        for copy in sends[h]:
            copy.wait_recv()
        spread(h)

        def body(i, carry):
            one(h, i)
            return carry

        lax.fori_loop(0, SIZE, body, 0, unroll=8)
        for a in range(parts):
            held = slice(a * chans + h * SIZE, a * chans + (h + 1) * SIZE)
            value = corr[held, :]
            value_hi = value.astype(jnp.bfloat16)
            r_out[a, h, :SIZE, :] = conv[held, :].astype(jnp.bfloat16)
            r_out[a, h, SIZE : 2 * SIZE, :] = value_hi
            r_out[a, h, 2 * SIZE :, :] = (value - value_hi.astype(jnp.float32)).astype(jnp.bfloat16)
        for k in far_first:
            to = others[k]
            returns.append(remote(r_out.at[to, h], r_in.at[me, h], r_send.at[h, k], r_recv.at[h, k], (section, to)))
            returns[-1].start()
    r_in[me] = r_out[me]
    for copy in returns:
        copy.wait_recv()

    for copy in sum(sends, g_sends + returns):
        copy.wait_send()


def finish_kernel(r_ref, ig_hbm, fg_hbm, ig_ref, fg_ref, sems):
    parts, chunks = r_ref.shape[:2]

    def gathered(kind):
        pieces = [
            r_ref[c, h, kind * SIZE : (kind + 1) * SIZE, :].astype(jnp.float32)
            for c in range(parts)
            for h in range(chunks)
        ]
        return jnp.concatenate(pieces, axis=0)

    store_fg = pltpu.make_async_copy(fg_ref, fg_hbm, sems.at[0])
    store_ig = pltpu.make_async_copy(ig_ref, ig_hbm, sems.at[1])
    fg_ref[...] = (gathered(1) + gathered(2)).T
    store_fg.start()
    ig_ref[...] = gathered(0).T.astype(jnp.bfloat16)
    store_ig.start()
    store_fg.wait()
    store_ig.wait()


def kernel_per_device(pipes, parts, layer_input, filters, skip, incoming, loss_grad):
    rows, width = loss_grad.shape
    chunks = width // parts // SIZE
    vmem = pl.BlockSpec(memory_space=pltpu.VMEM)
    hbm = pl.BlockSpec(memory_space=pl.ANY)
    narrow = pltpu.VMEM((width, rows), jnp.bfloat16)
    wide = pltpu.VMEM((width, rows), jnp.float32)
    triple = pltpu.VMEM((parts, chunks, 3 * SIZE, rows), jnp.bfloat16)
    sems = pltpu.SemaphoreType.DMA((chunks, parts))
    operands = (layer_input[0], filters[0], skip, incoming[0], loss_grad)
    returned = pl.pallas_call(
        functools.partial(correlate_kernel, pipes, parts),
        out_shape=pltpu.VMEM((parts, chunks, 3 * SIZE, rows), jnp.bfloat16),
        in_specs=[hbm] * 5,
        out_specs=vmem,
        scratch_shapes=[
            pltpu.VMEM((rows, width), jnp.bfloat16),
            pltpu.VMEM((rows, width), jnp.float32),
            pltpu.VMEM((rows, width), jnp.bfloat16),
            pltpu.SMEM((1, width), jnp.float32),
            triple,
            triple,
            narrow,
            narrow,
            pltpu.VMEM((parts * FINE // rows, 3 * (rows // FINE) * parts * SIZE, rows), jnp.float32),
            wide,
            wide,
            wide,
            triple,
            pltpu.SemaphoreType.DMA((4,)),
        ]
        + [sems] * 2
        + [pltpu.SemaphoreType.DMA((parts,))] * 2
        + [sems] * 2,
        compiler_params=pltpu.CompilerParams(
            collective_id=0, has_side_effects=True, vmem_limit_bytes=32 * 1024 * 1024
        ),
    )(*[pltpu.with_memory_space_constraint(operand, pltpu.HBM) for operand in operands])
    input_grad, filter_grad = pl.pallas_call(
        finish_kernel,
        out_shape=(
            jax.ShapeDtypeStruct((rows, width), jnp.bfloat16),
            jax.ShapeDtypeStruct((rows, width), jnp.float32),
        ),
        in_specs=[vmem],
        out_specs=(hbm, hbm),
        scratch_shapes=[
            pltpu.VMEM((rows, width), jnp.bfloat16),
            pltpu.VMEM((rows, width), jnp.float32),
            pltpu.SemaphoreType.DMA((2,)),
        ],
        compiler_params=pltpu.CompilerParams(vmem_limit_bytes=8 * 1024 * 1024),
    )(returned)
    return (input_grad[None], filter_grad[None])


def solution(mesh):
    pipes, parts = mesh.shape["pipe"], mesh.shape["seq"]

    def step(layer_input, filters, skip, incoming, loss_grad):
        rows, width = loss_grad.shape
        if pipes > 1 and parts == 8 and rows == 128 and width % (2 * SIZE * parts) == 0:
            return kernel_per_device(pipes, parts, layer_input, filters, skip, incoming, loss_grad)
        return per_device(layer_input, filters, skip, incoming, loss_grad)

    return jax.shard_map(
        step,
        mesh=mesh,
        in_specs=(
            P("pipe", "seq", None),
            P("pipe", "seq", None),
            P("pipe", None),
            P("pipe", "seq", None),
            P("seq", None),
        ),
        out_specs=(P("pipe", "seq", None), P("pipe", "seq", None)),
        check_vma=False,
    )
```

```python
import functools
import math

import jax
import jax.numpy as jnp
from jax import lax
from jax.experimental import pallas as pl
from jax.experimental.pallas import tpu as pltpu
from jax.sharding import PartitionSpec as P

MESH = pl.DeviceIdType.MESH
HIGHEST = lax.Precision.HIGHEST


def passed_along(block, axis, distance):
    devices = range(lax.axis_size(axis))
    route = [(i - distance, i) for i in devices if i - distance in devices]
    return lax.ppermute(block, axis, route)


def angle_table(left, right, modulus):
    product = left * right % modulus
    angle = product.astype(jnp.float32) * (2.0 * math.pi / modulus)
    return (jnp.cos(angle), jnp.sin(angle))


def forward_spectrum(signals):
    parts = lax.axis_size("seq")
    rows = signals.shape[1]
    block = rows // parts
    total = 2 * parts * rows
    place = lax.axis_index("seq")
    gathered = lax.all_to_all(signals[:, None], "seq", split_axis=2, concat_axis=1, tiled=True)
    freq_ids = lax.broadcasted_iota(jnp.int32, (2 * parts, parts), 0)
    class_ids = lax.broadcasted_iota(jnp.int32, (2 * parts, parts), 1)
    cos_tab, sin_tab = angle_table(freq_ids, class_ids, 2 * parts)
    real = jnp.einsum("rq,kqjc->krjc", cos_tab, gathered, precision=HIGHEST)
    imag = -jnp.einsum("rq,kqjc->krjc", sin_tab, gathered, precision=HIGHEST)
    freq_grid = lax.broadcasted_iota(jnp.int32, (1, 2 * parts, block, 1), 1)
    row_grid = place * block + lax.broadcasted_iota(jnp.int32, (1, 2 * parts, block, 1), 2)
    tw_cos, tw_sin = angle_table(freq_grid, row_grid, total)
    segment_real = real * tw_cos + imag * tw_sin
    segment_imag = imag * tw_cos - real * tw_sin
    real = lax.all_to_all(segment_real, "seq", split_axis=1, concat_axis=2, tiled=True)
    imag = lax.all_to_all(segment_imag, "seq", split_axis=1, concat_axis=2, tiled=True)
    out_ids = lax.broadcasted_iota(jnp.int32, (rows, rows), 0)
    row_ids = lax.broadcasted_iota(jnp.int32, (rows, rows), 1)
    cos_tab, sin_tab = angle_table(out_ids, row_ids, rows)
    out_real = jnp.einsum("sj,kmjc->kmsc", cos_tab, real, precision=HIGHEST) + jnp.einsum(
        "sj,kmjc->kmsc", sin_tab, imag, precision=HIGHEST
    )
    out_imag = jnp.einsum("sj,kmjc->kmsc", cos_tab, imag, precision=HIGHEST) - jnp.einsum(
        "sj,kmjc->kmsc", sin_tab, real, precision=HIGHEST
    )
    return (out_real, out_imag)


def inverse_signal(real, imag):
    parts = lax.axis_size("seq")
    rows = real.shape[2]
    total = 2 * parts * rows
    place = lax.axis_index("seq")
    row_ids = lax.broadcasted_iota(jnp.int32, (rows, rows), 0)
    out_ids = lax.broadcasted_iota(jnp.int32, (rows, rows), 1)
    cos_tab, sin_tab = angle_table(row_ids, out_ids, rows)
    part_real = jnp.einsum("js,kmsc->kmjc", cos_tab, real, precision=HIGHEST) - jnp.einsum(
        "js,kmsc->kmjc", sin_tab, imag, precision=HIGHEST
    )
    part_imag = jnp.einsum("js,kmsc->kmjc", sin_tab, real, precision=HIGHEST) + jnp.einsum(
        "js,kmsc->kmjc", cos_tab, imag, precision=HIGHEST
    )
    freq_grid = 2 * place + lax.broadcasted_iota(jnp.int32, (1, 2, rows, 1), 1)
    row_grid = lax.broadcasted_iota(jnp.int32, (1, 2, rows, 1), 2)
    tw_cos, tw_sin = angle_table(freq_grid, row_grid, total)
    turned_real = part_real * tw_cos - part_imag * tw_sin
    turned_imag = part_real * tw_sin + part_imag * tw_cos
    gath_real = lax.all_to_all(turned_real, "seq", split_axis=2, concat_axis=1, tiled=True)
    gath_imag = lax.all_to_all(turned_imag, "seq", split_axis=2, concat_axis=1, tiled=True)
    class_ids = lax.broadcasted_iota(jnp.int32, (parts, 2 * parts), 0)
    freq_ids = lax.broadcasted_iota(jnp.int32, (parts, 2 * parts), 1)
    cos_q, sin_q = angle_table(class_ids, freq_ids, 2 * parts)
    factor = 1.0 / total
    value_real = (
        jnp.einsum("qr,krjc->kqjc", cos_q, gath_real, precision=HIGHEST)
        - jnp.einsum("qr,krjc->kqjc", sin_q, gath_imag, precision=HIGHEST)
    ) * factor
    return lax.all_to_all(value_real, "seq", split_axis=1, concat_axis=2, tiled=True)


def per_device(layer_input, filters, skip, incoming, loss_grad):
    received = passed_along(incoming, "pipe", -1)
    is_last = lax.axis_index("pipe") == lax.axis_size("pipe") - 1
    grad_out = jnp.where(is_last, loss_grad[None], received)
    rows = layer_input.shape[1]
    seq_total = rows * lax.axis_size("seq")
    inputs = layer_input[0].astype(jnp.float32)
    grad_vals = grad_out[0].astype(jnp.float32)
    spec_real, spec_imag = forward_spectrum(jnp.stack([inputs, filters[0], grad_vals]))
    in_real, filt_real, grad_real = (spec_real[0], spec_real[1], spec_real[2])
    in_imag, filt_imag, grad_imag = (spec_imag[0], spec_imag[1], spec_imag[2])
    scale = 1.0 / math.sqrt(seq_total)
    adj_real = filt_real * grad_real + filt_imag * grad_imag
    adj_imag = filt_real * grad_imag - filt_imag * grad_real
    corr_real = (grad_real * in_real + grad_imag * in_imag) * scale
    corr_imag = (grad_imag * in_real - grad_real * in_imag) * scale
    results = inverse_signal(jnp.stack([adj_real, corr_real]), jnp.stack([adj_imag, corr_imag]))
    conv_grad = results[0, 0]
    filt_grad = results[1, 0]
    input_grad = (conv_grad + skip[0][None, :] * grad_vals).astype(jnp.bfloat16)
    return (input_grad[None], filt_grad[None])


SIZE = 16
FINE = 32


def remote(src, dst, send_sem, recv_sem, device):
    return pltpu.make_async_remote_copy(
        src_ref=src, dst_ref=dst, send_sem=send_sem, recv_sem=recv_sem, device_id=device, device_id_type=MESH
    )


def correlate_kernel(
    pipes, parts, x_hbm, f_hbm, skip_hbm, inc_hbm, loss_hbm, r_in,
    x_ref, f_ref, grad_ref, skip_ref, s_out, s_in, g_out, g_in, pads, g_val, conv, corr, r_out,
    load_sem, s_send, s_recv, g_send, g_recv, r_send, r_recv,
):
    section = lax.axis_index("pipe")
    me = lax.axis_index("seq")
    rows = x_ref.shape[0]
    chans = x_ref.shape[1] // parts
    chunks = chans // SIZE
    before = lax.rem(section + pipes - 1, pipes)
    after = lax.rem(section + 1, pipes)
    others = [lax.rem(me + k, parts) for k in range(parts)]

    @pl.when(section == 0)
    def _():
        pltpu.make_async_copy(loss_hbm, grad_ref, load_sem.at[0]).start()

    @pl.when(section != 0)
    def _():
        pltpu.make_async_copy(inc_hbm, grad_ref, load_sem.at[0]).start()

    load_f = pltpu.make_async_copy(f_hbm, f_ref, load_sem.at[1])
    load_x = pltpu.make_async_copy(x_hbm, x_ref, load_sem.at[2])
    load_skip = pltpu.make_async_copy(skip_hbm, skip_ref, load_sem.at[3])
    load_f.start()
    load_x.start()
    load_skip.start()

    barrier = pltpu.get_barrier_semaphore()
    for k in range(parts):
        if k:
            pl.semaphore_signal(barrier, inc=1, device_id=(section, others[k]), device_id_type=MESH)
        pl.semaphore_signal(barrier, inc=1, device_id=(after, others[k]), device_id_type=MESH)

    slot = parts - 1 - me

    def block_of(index):
        return pl.ds(pl.multiple_of(index * chans, SIZE), chans)

    pltpu.make_async_copy(inc_hbm, grad_ref, load_sem.at[0]).wait()
    g_out[...] = grad_ref[...].astype(jnp.float32).T.astype(jnp.bfloat16)

    row_ids = lax.broadcasted_iota(jnp.int32, (rows, rows), 0)
    col_ids = lax.broadcasted_iota(jnp.int32, (rows, rows), 1)
    flip = jnp.where(row_ids + col_ids == rows - 1, 1.0, 0.0).astype(jnp.bfloat16)

    def turned_over(block):
        return jnp.dot(flip, block, preferred_element_type=jnp.float32).T.astype(jnp.bfloat16)

    def place(kind, block):
        for c in range(parts):
            for h in range(chunks):
                start = c * chans + h * SIZE
                s_out[c, h, kind * SIZE : (kind + 1) * SIZE, :] = block[start : start + SIZE]

    load_f.wait()
    filt = f_ref[...]
    filt_hi = filt.astype(jnp.bfloat16)
    place(0, turned_over(filt_hi))
    place(1, turned_over((filt - filt_hi.astype(jnp.float32)).astype(jnp.bfloat16)))
    load_x.wait()
    place(2, turned_over(x_ref[...]))

    pl.semaphore_wait(barrier, 2 * parts - 1)

    sends, g_sends = [], []
    for h in range(chunks):
        group = []
        for k in range(1, parts + 1):
            to = others[k % parts]
            if k < parts:
                sems = (s_send.at[h, k], s_recv.at[h, k])
                group.append(remote(s_out.at[to, h], s_in.at[slot, h], *sems, (section, to)))
                group[-1].start()
            if h == 0:
                sems = (g_send.at[k % parts], g_recv.at[k % parts])
                g_sends.append(remote(g_out.at[block_of(to)], g_in.at[block_of(me)], *sems, (before, to)))
                g_sends[-1].start()
        sends.append(group)
    s_in[slot] = s_out[me]
    load_skip.wait()
    for copy in g_sends:
        copy.wait_recv()
    g_val[...] = g_in[...].astype(jnp.float32)

    groups = rows // FINE
    lane = lax.broadcasted_iota(jnp.int32, (3 * SIZE, rows), 1) // FINE
    fine_row = lax.broadcasted_iota(jnp.int32, (FINE, rows), 0)
    fine_col = lax.broadcasted_iota(jnp.int32, (FINE, rows), 1)
    keep = fine_col + FINE - 1 - fine_row < rows
    wide_lane = lax.broadcasted_iota(jnp.int32, (parts, rows), 1)
    tiles = parts // groups

    def spread(h):
        nothing = jnp.zeros((3 * SIZE, rows), jnp.bfloat16)
        turns = []
        for e in range(parts):
            block = s_in[e, h]
            turns.append([block] + [pltpu.roll(block, FINE * r, 1) for r in range(1, groups)])
        for j in range(groups):
            for a in range(parts):
                for v in range(tiles):
                    value = nothing
                    for q in range(groups):
                        e = groups * v + q + a
                        if e < parts:
                            value = jnp.where(lane == q, turns[e][(q - j) % groups], value)
                    value = value.astype(jnp.float32)
                    for kind in range(3):
                        start = ((kind * groups + j) * parts + a) * SIZE
                        pads[v, start : start + SIZE, :] = value[kind * SIZE : (kind + 1) * SIZE]

    def turned(chan, e):
        row = jnp.broadcast_to(g_val[pl.ds(e * chans + chan, 1), :].astype(jnp.bfloat16), (FINE, rows))
        return pltpu.roll(row, rows - FINE + 1, 1, stride=1, stride_axis=0)

    def one(h, i):
        chan = h * SIZE + i
        nothing = jnp.zeros((FINE, rows), jnp.bfloat16)
        turns = [turned(chan, e) for e in range(parts)] + [nothing]
        blocks = [jnp.where(keep, turns[e], turns[e + 1]) for e in range(parts)] + [nothing]
        right = jnp.concatenate(
            [jnp.concatenate([blocks[e], blocks[e + 1]], axis=1) for e in reversed(range(parts))], axis=0
        )
        left = jnp.concatenate(
            [
                jnp.concatenate(
                    [pads[v, pl.ds(m * parts * SIZE + i, parts, stride=SIZE), :] for v in range(tiles)], axis=1
                )
                for m in range(3 * groups)
            ],
            axis=0,
        )
        result = jnp.dot(left.astype(jnp.bfloat16), right, preferred_element_type=jnp.float32)

        def folded(kinds):
            total = None
            for j in range(groups):
                begin = FINE * (groups - 1 - j)
                part = sum(result[(kind * groups + j) * parts : (kind * groups + j + 1) * parts] for kind in kinds)
                piece = part[:, :rows]
                if begin:
                    piece = jnp.where(wide_lane >= begin, piece, part[:, rows:])
                    piece = pltpu.roll(piece, rows - begin, 1)
                total = piece if total is None else total + piece
            return total

        where = pl.ds(chan, parts, stride=chans)
        gain = skip_ref[0, me * chans + chan]
        conv[where, :] = folded((0, 1)) + gain * g_val[where, :]
        corr[where, :] = folded((2,)) * (1.0 / math.sqrt(rows * parts))

    returns = []
    for h in range(chunks):
        for copy in sends[h]:
            copy.wait_recv()
        spread(h)

        def body(i, carry):
            one(h, i)
            return carry

        lax.fori_loop(0, SIZE, body, 0, unroll=8)
        for a in range(parts):
            held = slice(a * chans + h * SIZE, a * chans + (h + 1) * SIZE)
            value = corr[held, :]
            value_hi = value.astype(jnp.bfloat16)
            r_out[a, h, :SIZE, :] = conv[held, :].astype(jnp.bfloat16)
            r_out[a, h, SIZE : 2 * SIZE, :] = value_hi
            r_out[a, h, 2 * SIZE :, :] = (value - value_hi.astype(jnp.float32)).astype(jnp.bfloat16)
        for k in range(1, parts):
            to = others[k]
            returns.append(remote(r_out.at[to, h], r_in.at[me, h], r_send.at[h, k], r_recv.at[h, k], (section, to)))
            returns[-1].start()
    r_in[me] = r_out[me]
    for copy in returns:
        copy.wait_recv()

    for copy in sum(sends, g_sends + returns):
        copy.wait_send()


def finish_kernel(r_ref, ig_hbm, fg_hbm, ig_ref, fg_ref, sems):
    parts, chunks = r_ref.shape[:2]

    def gathered(kind):
        pieces = [
            r_ref[c, h, kind * SIZE : (kind + 1) * SIZE, :].astype(jnp.float32)
            for c in range(parts)
            for h in range(chunks)
        ]
        return jnp.concatenate(pieces, axis=0)

    store_fg = pltpu.make_async_copy(fg_ref, fg_hbm, sems.at[0])
    store_ig = pltpu.make_async_copy(ig_ref, ig_hbm, sems.at[1])
    fg_ref[...] = (gathered(1) + gathered(2)).T
    store_fg.start()
    ig_ref[...] = gathered(0).T.astype(jnp.bfloat16)
    store_ig.start()
    store_fg.wait()
    store_ig.wait()


def kernel_per_device(pipes, parts, layer_input, filters, skip, incoming, loss_grad):
    rows, width = loss_grad.shape
    chunks = width // parts // SIZE
    vmem = pl.BlockSpec(memory_space=pltpu.VMEM)
    hbm = pl.BlockSpec(memory_space=pl.ANY)
    narrow = pltpu.VMEM((width, rows), jnp.bfloat16)
    wide = pltpu.VMEM((width, rows), jnp.float32)
    triple = pltpu.VMEM((parts, chunks, 3 * SIZE, rows), jnp.bfloat16)
    sems = pltpu.SemaphoreType.DMA((chunks, parts))
    operands = (layer_input[0], filters[0], skip, incoming[0], loss_grad)
    returned = pl.pallas_call(
        functools.partial(correlate_kernel, pipes, parts),
        out_shape=pltpu.VMEM((parts, chunks, 3 * SIZE, rows), jnp.bfloat16),
        in_specs=[hbm] * 5,
        out_specs=vmem,
        scratch_shapes=[
            pltpu.VMEM((rows, width), jnp.bfloat16),
            pltpu.VMEM((rows, width), jnp.float32),
            pltpu.VMEM((rows, width), jnp.bfloat16),
            pltpu.SMEM((1, width), jnp.float32),
            triple,
            triple,
            narrow,
            narrow,
            pltpu.VMEM((parts * FINE // rows, 3 * (rows // FINE) * parts * SIZE, rows), jnp.float32),
            wide,
            wide,
            wide,
            triple,
            pltpu.SemaphoreType.DMA((4,)),
        ]
        + [sems] * 2
        + [pltpu.SemaphoreType.DMA((parts,))] * 2
        + [sems] * 2,
        compiler_params=pltpu.CompilerParams(
            collective_id=0, has_side_effects=True, vmem_limit_bytes=32 * 1024 * 1024
        ),
    )(*[pltpu.with_memory_space_constraint(operand, pltpu.HBM) for operand in operands])
    input_grad, filter_grad = pl.pallas_call(
        finish_kernel,
        out_shape=(
            jax.ShapeDtypeStruct((rows, width), jnp.bfloat16),
            jax.ShapeDtypeStruct((rows, width), jnp.float32),
        ),
        in_specs=[vmem],
        out_specs=(hbm, hbm),
        scratch_shapes=[
            pltpu.VMEM((rows, width), jnp.bfloat16),
            pltpu.VMEM((rows, width), jnp.float32),
            pltpu.SemaphoreType.DMA((2,)),
        ],
        compiler_params=pltpu.CompilerParams(vmem_limit_bytes=8 * 1024 * 1024),
    )(returned)
    return (input_grad[None], filter_grad[None])


def solution(mesh):
    pipes, parts = mesh.shape["pipe"], mesh.shape["seq"]

    def step(layer_input, filters, skip, incoming, loss_grad):
        rows, width = loss_grad.shape
        if pipes > 1 and parts == 8 and rows == 128 and width % (2 * SIZE * parts) == 0:
            return kernel_per_device(pipes, parts, layer_input, filters, skip, incoming, loss_grad)
        return per_device(layer_input, filters, skip, incoming, loss_grad)

    return jax.shard_map(
        step,
        mesh=mesh,
        in_specs=(
            P("pipe", "seq", None),
            P("pipe", "seq", None),
            P("pipe", None),
            P("pipe", "seq", None),
            P("seq", None),
        ),
        out_specs=(P("pipe", "seq", None), P("pipe", "seq", None)),
        check_vma=False,
    )
```

```python
import functools
import math

import jax
import jax.numpy as jnp
from jax import lax
from jax.experimental import pallas as pl
from jax.experimental.pallas import tpu as pltpu
from jax.sharding import PartitionSpec as P

MESH = pl.DeviceIdType.MESH
HIGHEST = lax.Precision.HIGHEST


def passed_along(block, axis, distance):
    devices = range(lax.axis_size(axis))
    route = [(i - distance, i) for i in devices if i - distance in devices]
    return lax.ppermute(block, axis, route)


def angle_table(left, right, modulus):
    product = left * right % modulus
    angle = product.astype(jnp.float32) * (2.0 * math.pi / modulus)
    return (jnp.cos(angle), jnp.sin(angle))


def forward_spectrum(signals):
    parts = lax.axis_size("seq")
    rows = signals.shape[1]
    block = rows // parts
    total = 2 * parts * rows
    place = lax.axis_index("seq")
    gathered = lax.all_to_all(signals[:, None], "seq", split_axis=2, concat_axis=1, tiled=True)
    freq_ids = lax.broadcasted_iota(jnp.int32, (2 * parts, parts), 0)
    class_ids = lax.broadcasted_iota(jnp.int32, (2 * parts, parts), 1)
    cos_tab, sin_tab = angle_table(freq_ids, class_ids, 2 * parts)
    real = jnp.einsum("rq,kqjc->krjc", cos_tab, gathered, precision=HIGHEST)
    imag = -jnp.einsum("rq,kqjc->krjc", sin_tab, gathered, precision=HIGHEST)
    freq_grid = lax.broadcasted_iota(jnp.int32, (1, 2 * parts, block, 1), 1)
    row_grid = place * block + lax.broadcasted_iota(jnp.int32, (1, 2 * parts, block, 1), 2)
    tw_cos, tw_sin = angle_table(freq_grid, row_grid, total)
    segment_real = real * tw_cos + imag * tw_sin
    segment_imag = imag * tw_cos - real * tw_sin
    real = lax.all_to_all(segment_real, "seq", split_axis=1, concat_axis=2, tiled=True)
    imag = lax.all_to_all(segment_imag, "seq", split_axis=1, concat_axis=2, tiled=True)
    out_ids = lax.broadcasted_iota(jnp.int32, (rows, rows), 0)
    row_ids = lax.broadcasted_iota(jnp.int32, (rows, rows), 1)
    cos_tab, sin_tab = angle_table(out_ids, row_ids, rows)
    out_real = jnp.einsum("sj,kmjc->kmsc", cos_tab, real, precision=HIGHEST) + jnp.einsum(
        "sj,kmjc->kmsc", sin_tab, imag, precision=HIGHEST
    )
    out_imag = jnp.einsum("sj,kmjc->kmsc", cos_tab, imag, precision=HIGHEST) - jnp.einsum(
        "sj,kmjc->kmsc", sin_tab, real, precision=HIGHEST
    )
    return (out_real, out_imag)


def inverse_signal(real, imag):
    parts = lax.axis_size("seq")
    rows = real.shape[2]
    total = 2 * parts * rows
    place = lax.axis_index("seq")
    row_ids = lax.broadcasted_iota(jnp.int32, (rows, rows), 0)
    out_ids = lax.broadcasted_iota(jnp.int32, (rows, rows), 1)
    cos_tab, sin_tab = angle_table(row_ids, out_ids, rows)
    part_real = jnp.einsum("js,kmsc->kmjc", cos_tab, real, precision=HIGHEST) - jnp.einsum(
        "js,kmsc->kmjc", sin_tab, imag, precision=HIGHEST
    )
    part_imag = jnp.einsum("js,kmsc->kmjc", sin_tab, real, precision=HIGHEST) + jnp.einsum(
        "js,kmsc->kmjc", cos_tab, imag, precision=HIGHEST
    )
    freq_grid = 2 * place + lax.broadcasted_iota(jnp.int32, (1, 2, rows, 1), 1)
    row_grid = lax.broadcasted_iota(jnp.int32, (1, 2, rows, 1), 2)
    tw_cos, tw_sin = angle_table(freq_grid, row_grid, total)
    turned_real = part_real * tw_cos - part_imag * tw_sin
    turned_imag = part_real * tw_sin + part_imag * tw_cos
    gath_real = lax.all_to_all(turned_real, "seq", split_axis=2, concat_axis=1, tiled=True)
    gath_imag = lax.all_to_all(turned_imag, "seq", split_axis=2, concat_axis=1, tiled=True)
    class_ids = lax.broadcasted_iota(jnp.int32, (parts, 2 * parts), 0)
    freq_ids = lax.broadcasted_iota(jnp.int32, (parts, 2 * parts), 1)
    cos_q, sin_q = angle_table(class_ids, freq_ids, 2 * parts)
    factor = 1.0 / total
    value_real = (
        jnp.einsum("qr,krjc->kqjc", cos_q, gath_real, precision=HIGHEST)
        - jnp.einsum("qr,krjc->kqjc", sin_q, gath_imag, precision=HIGHEST)
    ) * factor
    return lax.all_to_all(value_real, "seq", split_axis=1, concat_axis=2, tiled=True)


def per_device(layer_input, filters, skip, incoming, loss_grad):
    received = passed_along(incoming, "pipe", -1)
    is_last = lax.axis_index("pipe") == lax.axis_size("pipe") - 1
    grad_out = jnp.where(is_last, loss_grad[None], received)
    rows = layer_input.shape[1]
    seq_total = rows * lax.axis_size("seq")
    inputs = layer_input[0].astype(jnp.float32)
    grad_vals = grad_out[0].astype(jnp.float32)
    spec_real, spec_imag = forward_spectrum(jnp.stack([inputs, filters[0], grad_vals]))
    in_real, filt_real, grad_real = (spec_real[0], spec_real[1], spec_real[2])
    in_imag, filt_imag, grad_imag = (spec_imag[0], spec_imag[1], spec_imag[2])
    scale = 1.0 / math.sqrt(seq_total)
    adj_real = filt_real * grad_real + filt_imag * grad_imag
    adj_imag = filt_real * grad_imag - filt_imag * grad_real
    corr_real = (grad_real * in_real + grad_imag * in_imag) * scale
    corr_imag = (grad_imag * in_real - grad_real * in_imag) * scale
    results = inverse_signal(jnp.stack([adj_real, corr_real]), jnp.stack([adj_imag, corr_imag]))
    conv_grad = results[0, 0]
    filt_grad = results[1, 0]
    input_grad = (conv_grad + skip[0][None, :] * grad_vals).astype(jnp.bfloat16)
    return (input_grad[None], filt_grad[None])


SIZE = 16
FINE = 32


def remote(src, dst, send_sem, recv_sem, device):
    return pltpu.make_async_remote_copy(
        src_ref=src, dst_ref=dst, send_sem=send_sem, recv_sem=recv_sem, device_id=device, device_id_type=MESH
    )


def correlate_kernel(
    pipes, parts, x_hbm, f_hbm, skip_hbm, inc_hbm, loss_hbm, r_in,
    x_ref, f_ref, grad_ref, skip_ref, s_out, s_in, g_out, g_in, pads, g_val, conv, corr, r_out,
    load_sem, s_send, s_recv, g_send, g_recv, r_send, r_recv,
):
    section = lax.axis_index("pipe")
    me = lax.axis_index("seq")
    rows = x_ref.shape[0]
    chans = x_ref.shape[1] // parts
    chunks = chans // SIZE
    before = lax.rem(section + pipes - 1, pipes)
    after = lax.rem(section + 1, pipes)
    others = [lax.rem(me + k, parts) for k in range(parts)]

    @pl.when(section == 0)
    def _():
        pltpu.make_async_copy(loss_hbm, grad_ref, load_sem.at[0]).start()

    @pl.when(section != 0)
    def _():
        pltpu.make_async_copy(inc_hbm, grad_ref, load_sem.at[0]).start()

    load_f = pltpu.make_async_copy(f_hbm, f_ref, load_sem.at[1])
    load_x = pltpu.make_async_copy(x_hbm, x_ref, load_sem.at[2])
    load_skip = pltpu.make_async_copy(skip_hbm, skip_ref, load_sem.at[3])
    load_f.start()
    load_x.start()
    load_skip.start()

    barrier = pltpu.get_barrier_semaphore()
    for k in range(parts):
        if k:
            pl.semaphore_signal(barrier, inc=1, device_id=(section, others[k]), device_id_type=MESH)
        pl.semaphore_signal(barrier, inc=1, device_id=(after, others[k]), device_id_type=MESH)

    row_ids = lax.broadcasted_iota(jnp.int32, (rows, rows), 0)
    col_ids = lax.broadcasted_iota(jnp.int32, (rows, rows), 1)
    flip = jnp.where(row_ids + col_ids == rows - 1, 1.0, 0.0).astype(jnp.bfloat16)

    def turned_over(block):
        return jnp.dot(flip, block, preferred_element_type=jnp.float32).T.astype(jnp.bfloat16)

    def place(kind, block):
        for c in range(parts):
            for h in range(chunks):
                start = c * chans + h * SIZE
                s_out[c, h, kind * SIZE : (kind + 1) * SIZE, :] = block[start : start + SIZE]

    pltpu.make_async_copy(inc_hbm, grad_ref, load_sem.at[0]).wait()
    g_out[...] = grad_ref[...].astype(jnp.float32).T.astype(jnp.bfloat16)
    load_f.wait()
    filt = f_ref[...]
    filt_hi = filt.astype(jnp.bfloat16)
    place(0, turned_over(filt_hi))
    place(1, turned_over((filt - filt_hi.astype(jnp.float32)).astype(jnp.bfloat16)))
    load_x.wait()
    place(2, turned_over(x_ref[...]))

    pl.semaphore_wait(barrier, 2 * parts - 1)

    def span(index, h):
        return pl.ds(pl.multiple_of(index * chans + h * SIZE, SIZE), SIZE)

    slot = parts - 1 - me
    sends = []
    for h in range(chunks):
        group = []
        for copy in sum(sends, []):
            copy.wait_send()
        for k in range(parts):
            to = others[k]
            sems = (g_send.at[h, k], g_recv.at[h, k])
            group.append(remote(g_out.at[span(to, h)], g_in.at[span(me, h)], *sems, (before, to)))
            group[-1].start()
            if k:
                sems = (s_send.at[h, k], s_recv.at[h, k])
                group.append(remote(s_out.at[to, h], s_in.at[slot, h], *sems, (section, to)))
                group[-1].start()
        sends.append(group)
    s_in[slot] = s_out[me]
    load_skip.wait()

    groups = rows // FINE
    lane = lax.broadcasted_iota(jnp.int32, (3 * SIZE, rows), 1) // FINE
    fine_row = lax.broadcasted_iota(jnp.int32, (FINE, rows), 0)
    fine_col = lax.broadcasted_iota(jnp.int32, (FINE, rows), 1)
    keep = fine_col + FINE - 1 - fine_row < rows
    wide_lane = lax.broadcasted_iota(jnp.int32, (parts, rows), 1)
    tiles = parts // groups

    def spread(h):
        nothing = jnp.zeros((3 * SIZE, rows), jnp.bfloat16)
        turns = []
        for e in range(parts):
            block = s_in[e, h]
            turns.append([block] + [pltpu.roll(block, FINE * r, 1) for r in range(1, groups)])
        for j in range(groups):
            for a in range(parts):
                for v in range(tiles):
                    value = nothing
                    for q in range(groups):
                        e = groups * v + q + a
                        if e < parts:
                            value = jnp.where(lane == q, turns[e][(q - j) % groups], value)
                    value = value.astype(jnp.float32)
                    for kind in range(3):
                        start = ((kind * groups + j) * parts + a) * SIZE
                        pads[v, start : start + SIZE, :] = value[kind * SIZE : (kind + 1) * SIZE]

    def turned(chan, e):
        row = jnp.broadcast_to(g_val[pl.ds(e * chans + chan, 1), :].astype(jnp.bfloat16), (FINE, rows))
        return pltpu.roll(row, rows - FINE + 1, 1, stride=1, stride_axis=0)

    def one(h, i):
        chan = h * SIZE + i
        nothing = jnp.zeros((FINE, rows), jnp.bfloat16)
        turns = [turned(chan, e) for e in range(parts)] + [nothing]
        blocks = [jnp.where(keep, turns[e], turns[e + 1]) for e in range(parts)] + [nothing]
        right = jnp.concatenate(
            [jnp.concatenate([blocks[e], blocks[e + 1]], axis=1) for e in reversed(range(parts))], axis=0
        )
        left = jnp.concatenate(
            [
                jnp.concatenate(
                    [pads[v, pl.ds(m * parts * SIZE + i, parts, stride=SIZE), :] for v in range(tiles)], axis=1
                )
                for m in range(3 * groups)
            ],
            axis=0,
        )
        result = jnp.dot(left.astype(jnp.bfloat16), right, preferred_element_type=jnp.float32)

        def folded(kinds):
            total = None
            for j in range(groups):
                begin = FINE * (groups - 1 - j)
                part = sum(result[(kind * groups + j) * parts : (kind * groups + j + 1) * parts] for kind in kinds)
                piece = part[:, :rows]
                if begin:
                    piece = jnp.where(wide_lane >= begin, piece, part[:, rows:])
                    piece = pltpu.roll(piece, rows - begin, 1)
                total = piece if total is None else total + piece
            return total

        where = pl.ds(chan, parts, stride=chans)
        gain = skip_ref[0, me * chans + chan]
        conv[where, :] = folded((0, 1)) + gain * g_val[where, :]
        corr[where, :] = folded((2,)) * (1.0 / math.sqrt(rows * parts))

    returns = []
    for h in range(chunks):
        for copy in sends[h]:
            copy.wait_recv()
        for e in range(parts):
            held = slice(e * chans + h * SIZE, e * chans + (h + 1) * SIZE)
            g_val[held, :] = g_in[held, :].astype(jnp.float32)
        spread(h)

        def body(i, carry):
            one(h, i)
            return carry

        lax.fori_loop(0, SIZE, body, 0, unroll=8)
        for a in range(parts):
            held = slice(a * chans + h * SIZE, a * chans + (h + 1) * SIZE)
            value = corr[held, :]
            value_hi = value.astype(jnp.bfloat16)
            r_out[a, h, :SIZE, :] = conv[held, :].astype(jnp.bfloat16)
            r_out[a, h, SIZE : 2 * SIZE, :] = value_hi
            r_out[a, h, 2 * SIZE :, :] = (value - value_hi.astype(jnp.float32)).astype(jnp.bfloat16)
        for k in range(1, parts):
            to = others[k]
            returns.append(remote(r_out.at[to, h], r_in.at[me, h], r_send.at[h, k], r_recv.at[h, k], (section, to)))
            returns[-1].start()
    r_in[me] = r_out[me]
    for copy in returns:
        copy.wait_recv()

    for copy in sends[-1] + returns:
        copy.wait_send()


def finish_kernel(r_ref, ig_hbm, fg_hbm, ig_ref, fg_ref, sems):
    parts, chunks = r_ref.shape[:2]

    def gathered(kind):
        pieces = [
            r_ref[c, h, kind * SIZE : (kind + 1) * SIZE, :].astype(jnp.float32)
            for c in range(parts)
            for h in range(chunks)
        ]
        return jnp.concatenate(pieces, axis=0)

    store_fg = pltpu.make_async_copy(fg_ref, fg_hbm, sems.at[0])
    store_ig = pltpu.make_async_copy(ig_ref, ig_hbm, sems.at[1])
    fg_ref[...] = (gathered(1) + gathered(2)).T
    store_fg.start()
    ig_ref[...] = gathered(0).T.astype(jnp.bfloat16)
    store_ig.start()
    store_fg.wait()
    store_ig.wait()


def kernel_per_device(pipes, parts, layer_input, filters, skip, incoming, loss_grad):
    rows, width = loss_grad.shape
    chunks = width // parts // SIZE
    vmem = pl.BlockSpec(memory_space=pltpu.VMEM)
    hbm = pl.BlockSpec(memory_space=pl.ANY)
    narrow = pltpu.VMEM((width, rows), jnp.bfloat16)
    wide = pltpu.VMEM((width, rows), jnp.float32)
    triple = pltpu.VMEM((parts, chunks, 3 * SIZE, rows), jnp.bfloat16)
    sems = pltpu.SemaphoreType.DMA((chunks, parts))
    operands = (layer_input[0], filters[0], skip, incoming[0], loss_grad)
    returned = pl.pallas_call(
        functools.partial(correlate_kernel, pipes, parts),
        out_shape=pltpu.VMEM((parts, chunks, 3 * SIZE, rows), jnp.bfloat16),
        in_specs=[hbm] * 5,
        out_specs=vmem,
        scratch_shapes=[
            pltpu.VMEM((rows, width), jnp.bfloat16),
            pltpu.VMEM((rows, width), jnp.float32),
            pltpu.VMEM((rows, width), jnp.bfloat16),
            pltpu.SMEM((1, width), jnp.float32),
            triple,
            triple,
            narrow,
            narrow,
            pltpu.VMEM((parts * FINE // rows, 3 * (rows // FINE) * parts * SIZE, rows), jnp.float32),
            wide,
            wide,
            wide,
            triple,
            pltpu.SemaphoreType.DMA((4,)),
        ]
        + [sems] * 6,
        compiler_params=pltpu.CompilerParams(
            collective_id=0, has_side_effects=True, vmem_limit_bytes=32 * 1024 * 1024
        ),
    )(*[pltpu.with_memory_space_constraint(operand, pltpu.HBM) for operand in operands])
    input_grad, filter_grad = pl.pallas_call(
        finish_kernel,
        out_shape=(
            jax.ShapeDtypeStruct((rows, width), jnp.bfloat16),
            jax.ShapeDtypeStruct((rows, width), jnp.float32),
        ),
        in_specs=[vmem],
        out_specs=(hbm, hbm),
        scratch_shapes=[
            pltpu.VMEM((rows, width), jnp.bfloat16),
            pltpu.VMEM((rows, width), jnp.float32),
            pltpu.SemaphoreType.DMA((2,)),
        ],
        compiler_params=pltpu.CompilerParams(vmem_limit_bytes=8 * 1024 * 1024),
    )(returned)
    return (input_grad[None], filter_grad[None])


def solution(mesh):
    pipes, parts = mesh.shape["pipe"], mesh.shape["seq"]

    def step(layer_input, filters, skip, incoming, loss_grad):
        rows, width = loss_grad.shape
        if pipes > 1 and parts == 8 and rows == 128 and width % (2 * SIZE * parts) == 0:
            return kernel_per_device(pipes, parts, layer_input, filters, skip, incoming, loss_grad)
        return per_device(layer_input, filters, skip, incoming, loss_grad)

    return jax.shard_map(
        step,
        mesh=mesh,
        in_specs=(
            P("pipe", "seq", None),
            P("pipe", "seq", None),
            P("pipe", None),
            P("pipe", "seq", None),
            P("seq", None),
        ),
        out_specs=(P("pipe", "seq", None), P("pipe", "seq", None)),
        check_vma=False,
    )
```

```python
import functools
import math

import jax
import jax.numpy as jnp
from jax import lax
from jax.experimental import pallas as pl
from jax.experimental.pallas import tpu as pltpu
from jax.sharding import PartitionSpec as P

MESH = pl.DeviceIdType.MESH
HIGHEST = lax.Precision.HIGHEST


def passed_along(block, axis, distance):
    devices = range(lax.axis_size(axis))
    route = [(i - distance, i) for i in devices if i - distance in devices]
    return lax.ppermute(block, axis, route)


def angle_table(left, right, modulus):
    product = left * right % modulus
    angle = product.astype(jnp.float32) * (2.0 * math.pi / modulus)
    return (jnp.cos(angle), jnp.sin(angle))


def forward_spectrum(signals):
    parts = lax.axis_size("seq")
    rows = signals.shape[1]
    block = rows // parts
    total = 2 * parts * rows
    place = lax.axis_index("seq")
    gathered = lax.all_to_all(signals[:, None], "seq", split_axis=2, concat_axis=1, tiled=True)
    freq_ids = lax.broadcasted_iota(jnp.int32, (2 * parts, parts), 0)
    class_ids = lax.broadcasted_iota(jnp.int32, (2 * parts, parts), 1)
    cos_tab, sin_tab = angle_table(freq_ids, class_ids, 2 * parts)
    real = jnp.einsum("rq,kqjc->krjc", cos_tab, gathered, precision=HIGHEST)
    imag = -jnp.einsum("rq,kqjc->krjc", sin_tab, gathered, precision=HIGHEST)
    freq_grid = lax.broadcasted_iota(jnp.int32, (1, 2 * parts, block, 1), 1)
    row_grid = place * block + lax.broadcasted_iota(jnp.int32, (1, 2 * parts, block, 1), 2)
    tw_cos, tw_sin = angle_table(freq_grid, row_grid, total)
    segment_real = real * tw_cos + imag * tw_sin
    segment_imag = imag * tw_cos - real * tw_sin
    real = lax.all_to_all(segment_real, "seq", split_axis=1, concat_axis=2, tiled=True)
    imag = lax.all_to_all(segment_imag, "seq", split_axis=1, concat_axis=2, tiled=True)
    out_ids = lax.broadcasted_iota(jnp.int32, (rows, rows), 0)
    row_ids = lax.broadcasted_iota(jnp.int32, (rows, rows), 1)
    cos_tab, sin_tab = angle_table(out_ids, row_ids, rows)
    out_real = jnp.einsum("sj,kmjc->kmsc", cos_tab, real, precision=HIGHEST) + jnp.einsum(
        "sj,kmjc->kmsc", sin_tab, imag, precision=HIGHEST
    )
    out_imag = jnp.einsum("sj,kmjc->kmsc", cos_tab, imag, precision=HIGHEST) - jnp.einsum(
        "sj,kmjc->kmsc", sin_tab, real, precision=HIGHEST
    )
    return (out_real, out_imag)


def inverse_signal(real, imag):
    parts = lax.axis_size("seq")
    rows = real.shape[2]
    total = 2 * parts * rows
    place = lax.axis_index("seq")
    row_ids = lax.broadcasted_iota(jnp.int32, (rows, rows), 0)
    out_ids = lax.broadcasted_iota(jnp.int32, (rows, rows), 1)
    cos_tab, sin_tab = angle_table(row_ids, out_ids, rows)
    part_real = jnp.einsum("js,kmsc->kmjc", cos_tab, real, precision=HIGHEST) - jnp.einsum(
        "js,kmsc->kmjc", sin_tab, imag, precision=HIGHEST
    )
    part_imag = jnp.einsum("js,kmsc->kmjc", sin_tab, real, precision=HIGHEST) + jnp.einsum(
        "js,kmsc->kmjc", cos_tab, imag, precision=HIGHEST
    )
    freq_grid = 2 * place + lax.broadcasted_iota(jnp.int32, (1, 2, rows, 1), 1)
    row_grid = lax.broadcasted_iota(jnp.int32, (1, 2, rows, 1), 2)
    tw_cos, tw_sin = angle_table(freq_grid, row_grid, total)
    turned_real = part_real * tw_cos - part_imag * tw_sin
    turned_imag = part_real * tw_sin + part_imag * tw_cos
    gath_real = lax.all_to_all(turned_real, "seq", split_axis=2, concat_axis=1, tiled=True)
    gath_imag = lax.all_to_all(turned_imag, "seq", split_axis=2, concat_axis=1, tiled=True)
    class_ids = lax.broadcasted_iota(jnp.int32, (parts, 2 * parts), 0)
    freq_ids = lax.broadcasted_iota(jnp.int32, (parts, 2 * parts), 1)
    cos_q, sin_q = angle_table(class_ids, freq_ids, 2 * parts)
    factor = 1.0 / total
    value_real = (
        jnp.einsum("qr,krjc->kqjc", cos_q, gath_real, precision=HIGHEST)
        - jnp.einsum("qr,krjc->kqjc", sin_q, gath_imag, precision=HIGHEST)
    ) * factor
    return lax.all_to_all(value_real, "seq", split_axis=1, concat_axis=2, tiled=True)


def per_device(layer_input, filters, skip, incoming, loss_grad):
    received = passed_along(incoming, "pipe", -1)
    is_last = lax.axis_index("pipe") == lax.axis_size("pipe") - 1
    grad_out = jnp.where(is_last, loss_grad[None], received)
    rows = layer_input.shape[1]
    seq_total = rows * lax.axis_size("seq")
    inputs = layer_input[0].astype(jnp.float32)
    grad_vals = grad_out[0].astype(jnp.float32)
    spec_real, spec_imag = forward_spectrum(jnp.stack([inputs, filters[0], grad_vals]))
    in_real, filt_real, grad_real = (spec_real[0], spec_real[1], spec_real[2])
    in_imag, filt_imag, grad_imag = (spec_imag[0], spec_imag[1], spec_imag[2])
    scale = 1.0 / math.sqrt(seq_total)
    adj_real = filt_real * grad_real + filt_imag * grad_imag
    adj_imag = filt_real * grad_imag - filt_imag * grad_real
    corr_real = (grad_real * in_real + grad_imag * in_imag) * scale
    corr_imag = (grad_imag * in_real - grad_real * in_imag) * scale
    results = inverse_signal(jnp.stack([adj_real, corr_real]), jnp.stack([adj_imag, corr_imag]))
    conv_grad = results[0, 0]
    filt_grad = results[1, 0]
    input_grad = (conv_grad + skip[0][None, :] * grad_vals).astype(jnp.bfloat16)
    return (input_grad[None], filt_grad[None])


SIZE = 16
FINE = 32


def remote(src, dst, send_sem, recv_sem, device):
    return pltpu.make_async_remote_copy(
        src_ref=src, dst_ref=dst, send_sem=send_sem, recv_sem=recv_sem, device_id=device, device_id_type=MESH
    )


def correlate_kernel(
    pipes, parts, x_hbm, f_hbm, skip_hbm, inc_hbm, loss_hbm, r_in,
    x_ref, f_ref, grad_ref, skip_ref, s_out, s_in, g_out, g_in, pads, g_val, conv, corr, r_out,
    load_sem, s_send, s_recv, g_send, g_recv, r_send, r_recv,
):
    section = lax.axis_index("pipe")
    me = lax.axis_index("seq")
    rows = x_ref.shape[0]
    chans = x_ref.shape[1] // parts
    chunks = chans // SIZE
    before = lax.rem(section + pipes - 1, pipes)
    after = lax.rem(section + 1, pipes)
    others = [lax.rem(me + k, parts) for k in range(parts)]

    @pl.when(section == 0)
    def _():
        pltpu.make_async_copy(loss_hbm, grad_ref, load_sem.at[0]).start()

    @pl.when(section != 0)
    def _():
        pltpu.make_async_copy(inc_hbm, grad_ref, load_sem.at[0]).start()

    load_f = pltpu.make_async_copy(f_hbm, f_ref, load_sem.at[1])
    load_x = pltpu.make_async_copy(x_hbm, x_ref, load_sem.at[2])
    load_skip = pltpu.make_async_copy(skip_hbm, skip_ref, load_sem.at[3])
    load_f.start()
    load_x.start()
    load_skip.start()

    barrier = pltpu.get_barrier_semaphore()
    for k in range(parts):
        if k:
            pl.semaphore_signal(barrier, inc=1, device_id=(section, others[k]), device_id_type=MESH)
        pl.semaphore_signal(barrier, inc=1, device_id=(after, others[k]), device_id_type=MESH)

    row_ids = lax.broadcasted_iota(jnp.int32, (rows, rows), 0)
    col_ids = lax.broadcasted_iota(jnp.int32, (rows, rows), 1)
    flip = jnp.where(row_ids + col_ids == rows - 1, 1.0, 0.0).astype(jnp.bfloat16)

    def turned_over(block):
        return jnp.dot(flip, block, preferred_element_type=jnp.float32).astype(jnp.bfloat16).T

    def place(kind, block):
        for c in range(parts):
            for h in range(chunks):
                start = c * chans + h * SIZE
                s_out[c, h, kind * SIZE : (kind + 1) * SIZE, :] = block[start : start + SIZE]

    pltpu.make_async_copy(inc_hbm, grad_ref, load_sem.at[0]).wait()
    g_out[...] = grad_ref[...].T
    load_f.wait()
    filt = f_ref[...]
    filt_hi = filt.astype(jnp.bfloat16)
    place(0, turned_over(filt_hi))
    place(1, turned_over((filt - filt_hi.astype(jnp.float32)).astype(jnp.bfloat16)))
    load_x.wait()
    place(2, turned_over(x_ref[...]))

    pl.semaphore_wait(barrier, 2 * parts - 1)

    def span(index, h):
        return pl.ds(pl.multiple_of(index * chans + h * SIZE, SIZE), SIZE)

    slot = parts - 1 - me
    sends = []
    for h in range(chunks):
        group = []
        for k in range(parts):
            to = others[k]
            sems = (g_send.at[h, k], g_recv.at[h, k])
            group.append(remote(g_out.at[span(to, h)], g_in.at[span(me, h)], *sems, (before, to)))
            group[-1].start()
            if k:
                sems = (s_send.at[h, k], s_recv.at[h, k])
                group.append(remote(s_out.at[to, h], s_in.at[slot, h], *sems, (section, to)))
                group[-1].start()
        sends.append(group)
    s_in[slot] = s_out[me]
    load_skip.wait()

    groups = rows // FINE
    lane = lax.broadcasted_iota(jnp.int32, (3 * SIZE, rows), 1) // FINE
    fine_row = lax.broadcasted_iota(jnp.int32, (FINE, rows), 0)
    fine_col = lax.broadcasted_iota(jnp.int32, (FINE, rows), 1)
    keep = fine_col + FINE - 1 - fine_row < rows
    wide_lane = lax.broadcasted_iota(jnp.int32, (parts, rows), 1)
    tiles = parts // groups

    def spread(h):
        nothing = jnp.zeros((3 * SIZE, rows), jnp.bfloat16)
        turns = []
        for e in range(parts):
            block = s_in[e, h]
            turns.append([block] + [pltpu.roll(block, FINE * r, 1) for r in range(1, groups)])
        for j in range(groups):
            for a in range(parts):
                for v in range(tiles):
                    value = nothing
                    for q in range(groups):
                        e = groups * v + q + a
                        if e < parts:
                            value = jnp.where(lane == q, turns[e][(q - j) % groups], value)
                    value = value.astype(jnp.float32)
                    for kind in range(3):
                        start = ((kind * groups + j) * parts + a) * SIZE
                        pads[v, start : start + SIZE, :] = value[kind * SIZE : (kind + 1) * SIZE]

    def turned(chan, e):
        row = jnp.broadcast_to(g_val[pl.ds(e * chans + chan, 1), :].astype(jnp.bfloat16), (FINE, rows))
        return pltpu.roll(row, rows - FINE + 1, 1, stride=1, stride_axis=0)

    def one(h, i):
        chan = h * SIZE + i
        nothing = jnp.zeros((FINE, rows), jnp.bfloat16)
        turns = [turned(chan, e) for e in range(parts)] + [nothing]
        blocks = [jnp.where(keep, turns[e], turns[e + 1]) for e in range(parts)] + [nothing]
        right = jnp.concatenate(
            [jnp.concatenate([blocks[e], blocks[e + 1]], axis=1) for e in reversed(range(parts))], axis=0
        )
        left = jnp.concatenate(
            [
                jnp.concatenate(
                    [pads[v, pl.ds(m * parts * SIZE + i, parts, stride=SIZE), :] for v in range(tiles)], axis=1
                )
                for m in range(3 * groups)
            ],
            axis=0,
        )
        result = jnp.dot(left.astype(jnp.bfloat16), right, preferred_element_type=jnp.float32)

        def folded(kinds):
            total = None
            for j in range(groups):
                begin = FINE * (groups - 1 - j)
                part = sum(result[(kind * groups + j) * parts : (kind * groups + j + 1) * parts] for kind in kinds)
                piece = part[:, :rows]
                if begin:
                    piece = jnp.where(wide_lane >= begin, piece, part[:, rows:])
                    piece = pltpu.roll(piece, rows - begin, 1)
                total = piece if total is None else total + piece
            return total

        where = pl.ds(chan, parts, stride=chans)
        gain = skip_ref[0, me * chans + chan]
        conv[where, :] = folded((0, 1)) + gain * g_val[where, :]
        corr[where, :] = folded((2,)) * (1.0 / math.sqrt(rows * parts))

    returns = []
    for h in range(chunks):
        for copy in sends[h]:
            copy.wait_recv()
        for e in range(parts):
            held = slice(e * chans + h * SIZE, e * chans + (h + 1) * SIZE)
            g_val[held, :] = g_in[held, :].astype(jnp.float32)
        spread(h)

        def body(i, carry):
            one(h, i)
            return carry

        lax.fori_loop(0, SIZE, body, 0, unroll=16)
        for a in range(parts):
            held = slice(a * chans + h * SIZE, a * chans + (h + 1) * SIZE)
            value = corr[held, :]
            value_hi = value.astype(jnp.bfloat16)
            r_out[a, h, :SIZE, :] = conv[held, :].astype(jnp.bfloat16)
            r_out[a, h, SIZE : 2 * SIZE, :] = value_hi
            r_out[a, h, 2 * SIZE :, :] = (value - value_hi.astype(jnp.float32)).astype(jnp.bfloat16)
        for k in range(1, parts):
            to = others[k]
            returns.append(remote(r_out.at[to, h], r_in.at[me, h], r_send.at[h, k], r_recv.at[h, k], (section, to)))
            returns[-1].start()
    r_in[me] = r_out[me]
    for copy in returns:
        copy.wait_recv()

    for copy in sum(sends, returns):
        copy.wait_send()


def finish_kernel(r_ref, ig_hbm, fg_hbm, ig_ref, fg_ref, sems):
    parts, chunks = r_ref.shape[:2]

    def gathered(kind):
        pieces = [
            r_ref[c, h, kind * SIZE : (kind + 1) * SIZE, :]
            for c in range(parts)
            for h in range(chunks)
        ]
        return jnp.concatenate(pieces, axis=0)

    store_fg = pltpu.make_async_copy(fg_ref, fg_hbm, sems.at[0])
    store_ig = pltpu.make_async_copy(ig_ref, ig_hbm, sems.at[1])
    fg_ref[...] = (gathered(1).astype(jnp.float32) + gathered(2).astype(jnp.float32)).T
    store_fg.start()
    ig_ref[...] = gathered(0).T
    store_ig.start()
    store_fg.wait()
    store_ig.wait()


def kernel_per_device(pipes, parts, layer_input, filters, skip, incoming, loss_grad):
    rows, width = loss_grad.shape
    chunks = width // parts // SIZE
    vmem = pl.BlockSpec(memory_space=pltpu.VMEM)
    hbm = pl.BlockSpec(memory_space=pl.ANY)
    narrow = pltpu.VMEM((width, rows), jnp.bfloat16)
    wide = pltpu.VMEM((width, rows), jnp.float32)
    triple = pltpu.VMEM((parts, chunks, 3 * SIZE, rows), jnp.bfloat16)
    sems = pltpu.SemaphoreType.DMA((chunks, parts))
    operands = (layer_input[0], filters[0], skip, incoming[0], loss_grad)
    returned = pl.pallas_call(
        functools.partial(correlate_kernel, pipes, parts),
        out_shape=pltpu.VMEM((parts, chunks, 3 * SIZE, rows), jnp.bfloat16),
        in_specs=[hbm] * 5,
        out_specs=vmem,
        scratch_shapes=[
            pltpu.VMEM((rows, width), jnp.bfloat16),
            pltpu.VMEM((rows, width), jnp.float32),
            pltpu.VMEM((rows, width), jnp.bfloat16),
            pltpu.SMEM((1, width), jnp.float32),
            triple,
            triple,
            narrow,
            narrow,
            pltpu.VMEM((parts * FINE // rows, 3 * (rows // FINE) * parts * SIZE, rows), jnp.float32),
            wide,
            wide,
            wide,
            triple,
            pltpu.SemaphoreType.DMA((4,)),
        ]
        + [sems] * 6,
        compiler_params=pltpu.CompilerParams(
            collective_id=0, has_side_effects=True, vmem_limit_bytes=32 * 1024 * 1024
        ),
    )(*[pltpu.with_memory_space_constraint(operand, pltpu.HBM) for operand in operands])
    input_grad, filter_grad = pl.pallas_call(
        finish_kernel,
        out_shape=(
            jax.ShapeDtypeStruct((rows, width), jnp.bfloat16),
            jax.ShapeDtypeStruct((rows, width), jnp.float32),
        ),
        in_specs=[vmem],
        out_specs=(hbm, hbm),
        scratch_shapes=[
            pltpu.VMEM((rows, width), jnp.bfloat16),
            pltpu.VMEM((rows, width), jnp.float32),
            pltpu.SemaphoreType.DMA((2,)),
        ],
        compiler_params=pltpu.CompilerParams(vmem_limit_bytes=8 * 1024 * 1024),
    )(returned)
    return (input_grad[None], filter_grad[None])


def solution(mesh):
    pipes, parts = mesh.shape["pipe"], mesh.shape["seq"]

    def step(layer_input, filters, skip, incoming, loss_grad):
        rows, width = loss_grad.shape
        if pipes > 1 and parts == 8 and rows == 128 and width % (2 * SIZE * parts) == 0:
            return kernel_per_device(pipes, parts, layer_input, filters, skip, incoming, loss_grad)
        return per_device(layer_input, filters, skip, incoming, loss_grad)

    return jax.shard_map(
        step,
        mesh=mesh,
        in_specs=(
            P("pipe", "seq", None),
            P("pipe", "seq", None),
            P("pipe", None),
            P("pipe", "seq", None),
            P("seq", None),
        ),
        out_specs=(P("pipe", "seq", None), P("pipe", "seq", None)),
        check_vma=False,
    )
```

```python
import functools
import math

import jax
import jax.numpy as jnp
from jax import lax
from jax.experimental import pallas as pl
from jax.experimental.pallas import tpu as pltpu
from jax.sharding import PartitionSpec as P

MESH = pl.DeviceIdType.MESH
HIGHEST = lax.Precision.HIGHEST


def passed_along(block, axis, distance):
    devices = range(lax.axis_size(axis))
    route = [(i - distance, i) for i in devices if i - distance in devices]
    return lax.ppermute(block, axis, route)


def angle_table(left, right, modulus):
    product = left * right % modulus
    angle = product.astype(jnp.float32) * (2.0 * math.pi / modulus)
    return (jnp.cos(angle), jnp.sin(angle))


def forward_spectrum(signals):
    parts = lax.axis_size("seq")
    rows = signals.shape[1]
    block = rows // parts
    total = 2 * parts * rows
    place = lax.axis_index("seq")
    gathered = lax.all_to_all(signals[:, None], "seq", split_axis=2, concat_axis=1, tiled=True)
    freq_ids = lax.broadcasted_iota(jnp.int32, (2 * parts, parts), 0)
    class_ids = lax.broadcasted_iota(jnp.int32, (2 * parts, parts), 1)
    cos_tab, sin_tab = angle_table(freq_ids, class_ids, 2 * parts)
    real = jnp.einsum("rq,kqjc->krjc", cos_tab, gathered, precision=HIGHEST)
    imag = -jnp.einsum("rq,kqjc->krjc", sin_tab, gathered, precision=HIGHEST)
    freq_grid = lax.broadcasted_iota(jnp.int32, (1, 2 * parts, block, 1), 1)
    row_grid = place * block + lax.broadcasted_iota(jnp.int32, (1, 2 * parts, block, 1), 2)
    tw_cos, tw_sin = angle_table(freq_grid, row_grid, total)
    segment_real = real * tw_cos + imag * tw_sin
    segment_imag = imag * tw_cos - real * tw_sin
    real = lax.all_to_all(segment_real, "seq", split_axis=1, concat_axis=2, tiled=True)
    imag = lax.all_to_all(segment_imag, "seq", split_axis=1, concat_axis=2, tiled=True)
    out_ids = lax.broadcasted_iota(jnp.int32, (rows, rows), 0)
    row_ids = lax.broadcasted_iota(jnp.int32, (rows, rows), 1)
    cos_tab, sin_tab = angle_table(out_ids, row_ids, rows)
    out_real = jnp.einsum("sj,kmjc->kmsc", cos_tab, real, precision=HIGHEST) + jnp.einsum(
        "sj,kmjc->kmsc", sin_tab, imag, precision=HIGHEST
    )
    out_imag = jnp.einsum("sj,kmjc->kmsc", cos_tab, imag, precision=HIGHEST) - jnp.einsum(
        "sj,kmjc->kmsc", sin_tab, real, precision=HIGHEST
    )
    return (out_real, out_imag)


def inverse_signal(real, imag):
    parts = lax.axis_size("seq")
    rows = real.shape[2]
    total = 2 * parts * rows
    place = lax.axis_index("seq")
    row_ids = lax.broadcasted_iota(jnp.int32, (rows, rows), 0)
    out_ids = lax.broadcasted_iota(jnp.int32, (rows, rows), 1)
    cos_tab, sin_tab = angle_table(row_ids, out_ids, rows)
    part_real = jnp.einsum("js,kmsc->kmjc", cos_tab, real, precision=HIGHEST) - jnp.einsum(
        "js,kmsc->kmjc", sin_tab, imag, precision=HIGHEST
    )
    part_imag = jnp.einsum("js,kmsc->kmjc", sin_tab, real, precision=HIGHEST) + jnp.einsum(
        "js,kmsc->kmjc", cos_tab, imag, precision=HIGHEST
    )
    freq_grid = 2 * place + lax.broadcasted_iota(jnp.int32, (1, 2, rows, 1), 1)
    row_grid = lax.broadcasted_iota(jnp.int32, (1, 2, rows, 1), 2)
    tw_cos, tw_sin = angle_table(freq_grid, row_grid, total)
    turned_real = part_real * tw_cos - part_imag * tw_sin
    turned_imag = part_real * tw_sin + part_imag * tw_cos
    gath_real = lax.all_to_all(turned_real, "seq", split_axis=2, concat_axis=1, tiled=True)
    gath_imag = lax.all_to_all(turned_imag, "seq", split_axis=2, concat_axis=1, tiled=True)
    class_ids = lax.broadcasted_iota(jnp.int32, (parts, 2 * parts), 0)
    freq_ids = lax.broadcasted_iota(jnp.int32, (parts, 2 * parts), 1)
    cos_q, sin_q = angle_table(class_ids, freq_ids, 2 * parts)
    factor = 1.0 / total
    value_real = (
        jnp.einsum("qr,krjc->kqjc", cos_q, gath_real, precision=HIGHEST)
        - jnp.einsum("qr,krjc->kqjc", sin_q, gath_imag, precision=HIGHEST)
    ) * factor
    return lax.all_to_all(value_real, "seq", split_axis=1, concat_axis=2, tiled=True)


def per_device(layer_input, filters, skip, incoming, loss_grad):
    received = passed_along(incoming, "pipe", -1)
    is_last = lax.axis_index("pipe") == lax.axis_size("pipe") - 1
    grad_out = jnp.where(is_last, loss_grad[None], received)
    rows = layer_input.shape[1]
    seq_total = rows * lax.axis_size("seq")
    inputs = layer_input[0].astype(jnp.float32)
    grad_vals = grad_out[0].astype(jnp.float32)
    spec_real, spec_imag = forward_spectrum(jnp.stack([inputs, filters[0], grad_vals]))
    in_real, filt_real, grad_real = (spec_real[0], spec_real[1], spec_real[2])
    in_imag, filt_imag, grad_imag = (spec_imag[0], spec_imag[1], spec_imag[2])
    scale = 1.0 / math.sqrt(seq_total)
    adj_real = filt_real * grad_real + filt_imag * grad_imag
    adj_imag = filt_real * grad_imag - filt_imag * grad_real
    corr_real = (grad_real * in_real + grad_imag * in_imag) * scale
    corr_imag = (grad_imag * in_real - grad_real * in_imag) * scale
    results = inverse_signal(jnp.stack([adj_real, corr_real]), jnp.stack([adj_imag, corr_imag]))
    conv_grad = results[0, 0]
    filt_grad = results[1, 0]
    input_grad = (conv_grad + skip[0][None, :] * grad_vals).astype(jnp.bfloat16)
    return (input_grad[None], filt_grad[None])


SIZE = 16
FINE = 32


def remote(src, dst, send_sem, recv_sem, device):
    return pltpu.make_async_remote_copy(
        src_ref=src, dst_ref=dst, send_sem=send_sem, recv_sem=recv_sem, device_id=device, device_id_type=MESH
    )


def correlate_kernel(
    pipes, parts, x_hbm, f_hbm, skip_hbm, inc_hbm, loss_hbm, r_in,
    x_ref, f_ref, grad_ref, skip_ref, s_out, s_in, g_out, g_in, pads, g_val, conv, corr, r_out,
    load_sem, s_send, s_recv, g_send, g_recv, r_send, r_recv,
):
    section = lax.axis_index("pipe")
    me = lax.axis_index("seq")
    rows = x_ref.shape[0]
    chans = x_ref.shape[1] // parts
    chunks = chans // SIZE
    before = lax.rem(section + pipes - 1, pipes)
    after = lax.rem(section + 1, pipes)
    bits = [2**b for b in range(parts.bit_length() - 1)]
    others = [sum(lax.rem(me // b + k // b, 2) * b for b in bits) for k in range(parts)]

    @pl.when(section == 0)
    def _():
        pltpu.make_async_copy(loss_hbm, grad_ref, load_sem.at[0]).start()

    @pl.when(section != 0)
    def _():
        pltpu.make_async_copy(inc_hbm, grad_ref, load_sem.at[0]).start()

    load_f = pltpu.make_async_copy(f_hbm, f_ref, load_sem.at[1])
    load_x = pltpu.make_async_copy(x_hbm, x_ref, load_sem.at[2])
    load_skip = pltpu.make_async_copy(skip_hbm, skip_ref, load_sem.at[3])
    load_f.start()
    load_x.start()
    load_skip.start()

    barrier = pltpu.get_barrier_semaphore()
    for k in range(parts):
        if k:
            pl.semaphore_signal(barrier, inc=1, device_id=(section, others[k]), device_id_type=MESH)
        pl.semaphore_signal(barrier, inc=1, device_id=(after, others[k]), device_id_type=MESH)

    row_ids = lax.broadcasted_iota(jnp.int32, (rows, rows), 0)
    col_ids = lax.broadcasted_iota(jnp.int32, (rows, rows), 1)
    flip = jnp.where(row_ids + col_ids == rows - 1, 1.0, 0.0).astype(jnp.bfloat16)

    def turned_over(block):
        return jnp.dot(flip, block, preferred_element_type=jnp.float32).astype(jnp.bfloat16).T

    def place(kind, block):
        for c in range(parts):
            for h in range(chunks):
                start = c * chans + h * SIZE
                s_out[c, h, kind * SIZE : (kind + 1) * SIZE, :] = block[start : start + SIZE]

    pltpu.make_async_copy(inc_hbm, grad_ref, load_sem.at[0]).wait()
    g_out[...] = grad_ref[...].T
    load_f.wait()
    filt = f_ref[...]
    filt_hi = filt.astype(jnp.bfloat16)
    place(0, turned_over(filt_hi))
    place(1, turned_over((filt - filt_hi.astype(jnp.float32)).astype(jnp.bfloat16)))
    load_x.wait()
    place(2, turned_over(x_ref[...]))

    pl.semaphore_wait(barrier, 2 * parts - 1)

    def span(index, h):
        return pl.ds(pl.multiple_of(index * chans + h * SIZE, SIZE), SIZE)

    slot = parts - 1 - me
    sends = []
    for h in range(chunks):
        group = []
        for k in range(parts):
            to = others[k]
            sems = (g_send.at[h, k], g_recv.at[h, k])
            group.append(remote(g_out.at[span(to, h)], g_in.at[span(me, h)], *sems, (before, to)))
            group[-1].start()
            if k:
                sems = (s_send.at[h, k], s_recv.at[h, k])
                group.append(remote(s_out.at[to, h], s_in.at[slot, h], *sems, (section, to)))
                group[-1].start()
        sends.append(group)
    s_in[slot] = s_out[me]
    load_skip.wait()

    groups = rows // FINE
    lane = lax.broadcasted_iota(jnp.int32, (3 * SIZE, rows), 1) // FINE
    fine_row = lax.broadcasted_iota(jnp.int32, (FINE, rows), 0)
    fine_col = lax.broadcasted_iota(jnp.int32, (FINE, rows), 1)
    keep = fine_col + FINE - 1 - fine_row < rows
    wide_lane = lax.broadcasted_iota(jnp.int32, (parts, rows), 1)
    tiles = parts // groups

    def spread(h):
        nothing = jnp.zeros((3 * SIZE, rows), jnp.bfloat16)
        turns = []
        for e in range(parts):
            block = s_in[e, h]
            turns.append([block] + [pltpu.roll(block, FINE * r, 1) for r in range(1, groups)])
        for j in range(groups):
            for a in range(parts):
                for v in range(tiles):
                    value = nothing
                    for q in range(groups):
                        e = groups * v + q + a
                        if e < parts:
                            value = jnp.where(lane == q, turns[e][(q - j) % groups], value)
                    value = value.astype(jnp.float32)
                    for kind in range(3):
                        start = ((kind * groups + j) * parts + a) * SIZE
                        pads[v, start : start + SIZE, :] = value[kind * SIZE : (kind + 1) * SIZE]

    def turned(chan, e):
        row = jnp.broadcast_to(g_val[pl.ds(e * chans + chan, 1), :].astype(jnp.bfloat16), (FINE, rows))
        return pltpu.roll(row, rows - FINE + 1, 1, stride=1, stride_axis=0)

    def one(h, i):
        chan = h * SIZE + i
        nothing = jnp.zeros((FINE, rows), jnp.bfloat16)
        turns = [turned(chan, e) for e in range(parts)] + [nothing]
        blocks = [jnp.where(keep, turns[e], turns[e + 1]) for e in range(parts)] + [nothing]
        right = jnp.concatenate(
            [jnp.concatenate([blocks[e], blocks[e + 1]], axis=1) for e in reversed(range(parts))], axis=0
        )
        left = jnp.concatenate(
            [
                jnp.concatenate(
                    [pads[v, pl.ds(m * parts * SIZE + i, parts, stride=SIZE), :] for v in range(tiles)], axis=1
                )
                for m in range(3 * groups)
            ],
            axis=0,
        )
        result = jnp.dot(left.astype(jnp.bfloat16), right, preferred_element_type=jnp.float32)

        def folded(kinds):
            total = None
            for j in range(groups):
                begin = FINE * (groups - 1 - j)
                part = sum(result[(kind * groups + j) * parts : (kind * groups + j + 1) * parts] for kind in kinds)
                piece = part[:, :rows]
                if begin:
                    piece = jnp.where(wide_lane >= begin, piece, part[:, rows:])
                    piece = pltpu.roll(piece, rows - begin, 1)
                total = piece if total is None else total + piece
            return total

        where = pl.ds(chan, parts, stride=chans)
        gain = skip_ref[0, me * chans + chan]
        conv[where, :] = folded((0, 1)) + gain * g_val[where, :]
        corr[where, :] = folded((2,)) * (1.0 / math.sqrt(rows * parts))

    returns = []
    for h in range(chunks):
        for copy in sends[h]:
            copy.wait_recv()
        for e in range(parts):
            held = slice(e * chans + h * SIZE, e * chans + (h + 1) * SIZE)
            g_val[held, :] = g_in[held, :].astype(jnp.float32)
        spread(h)

        def body(i, carry):
            one(h, i)
            return carry

        lax.fori_loop(0, SIZE, body, 0, unroll=16)
        for a in range(parts):
            held = slice(a * chans + h * SIZE, a * chans + (h + 1) * SIZE)
            value = corr[held, :]
            value_hi = value.astype(jnp.bfloat16)
            r_out[a, h, :SIZE, :] = conv[held, :].astype(jnp.bfloat16)
            r_out[a, h, SIZE : 2 * SIZE, :] = value_hi
            r_out[a, h, 2 * SIZE :, :] = (value - value_hi.astype(jnp.float32)).astype(jnp.bfloat16)
        for k in range(1, parts):
            to = others[k]
            returns.append(remote(r_out.at[to, h], r_in.at[me, h], r_send.at[h, k], r_recv.at[h, k], (section, to)))
            returns[-1].start()
    r_in[me] = r_out[me]
    for copy in returns:
        copy.wait_recv()

    for copy in sum(sends, returns):
        copy.wait_send()


def finish_kernel(r_ref, ig_hbm, fg_hbm, ig_ref, fg_ref, sems):
    parts, chunks = r_ref.shape[:2]

    def gathered(kind):
        pieces = [
            r_ref[c, h, kind * SIZE : (kind + 1) * SIZE, :]
            for c in range(parts)
            for h in range(chunks)
        ]
        return jnp.concatenate(pieces, axis=0)

    store_fg = pltpu.make_async_copy(fg_ref, fg_hbm, sems.at[0])
    store_ig = pltpu.make_async_copy(ig_ref, ig_hbm, sems.at[1])
    fg_ref[...] = (gathered(1).astype(jnp.float32) + gathered(2).astype(jnp.float32)).T
    store_fg.start()
    ig_ref[...] = gathered(0).T
    store_ig.start()
    store_fg.wait()
    store_ig.wait()


def kernel_per_device(pipes, parts, layer_input, filters, skip, incoming, loss_grad):
    rows, width = loss_grad.shape
    chunks = width // parts // SIZE
    vmem = pl.BlockSpec(memory_space=pltpu.VMEM)
    hbm = pl.BlockSpec(memory_space=pl.ANY)
    narrow = pltpu.VMEM((width, rows), jnp.bfloat16)
    wide = pltpu.VMEM((width, rows), jnp.float32)
    triple = pltpu.VMEM((parts, chunks, 3 * SIZE, rows), jnp.bfloat16)
    sems = pltpu.SemaphoreType.DMA((chunks, parts))
    operands = (layer_input[0], filters[0], skip, incoming[0], loss_grad)
    returned = pl.pallas_call(
        functools.partial(correlate_kernel, pipes, parts),
        out_shape=pltpu.VMEM((parts, chunks, 3 * SIZE, rows), jnp.bfloat16),
        in_specs=[hbm] * 5,
        out_specs=vmem,
        scratch_shapes=[
            pltpu.VMEM((rows, width), jnp.bfloat16),
            pltpu.VMEM((rows, width), jnp.float32),
            pltpu.VMEM((rows, width), jnp.bfloat16),
            pltpu.SMEM((1, width), jnp.float32),
            triple,
            triple,
            narrow,
            narrow,
            pltpu.VMEM((parts * FINE // rows, 3 * (rows // FINE) * parts * SIZE, rows), jnp.float32),
            wide,
            wide,
            wide,
            triple,
            pltpu.SemaphoreType.DMA((4,)),
        ]
        + [sems] * 6,
        compiler_params=pltpu.CompilerParams(
            collective_id=0, has_side_effects=True, vmem_limit_bytes=32 * 1024 * 1024
        ),
    )(*[pltpu.with_memory_space_constraint(operand, pltpu.HBM) for operand in operands])
    input_grad, filter_grad = pl.pallas_call(
        finish_kernel,
        out_shape=(
            jax.ShapeDtypeStruct((rows, width), jnp.bfloat16),
            jax.ShapeDtypeStruct((rows, width), jnp.float32),
        ),
        in_specs=[vmem],
        out_specs=(hbm, hbm),
        scratch_shapes=[
            pltpu.VMEM((rows, width), jnp.bfloat16),
            pltpu.VMEM((rows, width), jnp.float32),
            pltpu.SemaphoreType.DMA((2,)),
        ],
        compiler_params=pltpu.CompilerParams(vmem_limit_bytes=8 * 1024 * 1024),
    )(returned)
    return (input_grad[None], filter_grad[None])


def solution(mesh):
    pipes, parts = mesh.shape["pipe"], mesh.shape["seq"]

    def step(layer_input, filters, skip, incoming, loss_grad):
        rows, width = loss_grad.shape
        if pipes > 1 and parts == 8 and rows == 128 and width % (2 * SIZE * parts) == 0:
            return kernel_per_device(pipes, parts, layer_input, filters, skip, incoming, loss_grad)
        return per_device(layer_input, filters, skip, incoming, loss_grad)

    return jax.shard_map(
        step,
        mesh=mesh,
        in_specs=(
            P("pipe", "seq", None),
            P("pipe", "seq", None),
            P("pipe", None),
            P("pipe", "seq", None),
            P("seq", None),
        ),
        out_specs=(P("pipe", "seq", None), P("pipe", "seq", None)),
        check_vma=False,
    )
```
